512 devices in a mesh: ctx: 32 (over y, x), tp: 16 (over z, core).
Axes of the slice: x: 4, y: 8, z: 8, core: 2. Of those that a mesh axis runs over, the one named last changes fastest.
Arguments:
- hidden_states: bfloat16 [8192, 8192], P('ctx', 'tp'), may hold values from -6 to 6
- ssm_input: bfloat16 [8192, 16384], P('ctx', 'tp'), may hold values from -6 to 6
- step_size: float32 [256, 8192], P('tp', 'ctx'), may hold values from 0.25 to 73728
- decay_rate: float32 [256], P('tp'), may hold values from 6.1035156e-06 to 0.05
- proj_b: bfloat16 [16, 8192], P(None, 'ctx'), may hold values from -1.5 to 1.5
- proj_c: bfloat16 [16, 8192], P(None, 'ctx'), may hold values from -1.5 to 1.5
- skip_gain: float32 [256], P('tp'), may hold values from 0.5 to 2
- norm_gain: float32 [16384], P('tp'), may hold values from 0.5 to 1.5
- latent_from_ssm: bfloat16 [16384, 256], P('tp'), may hold values from -0.03125 to 0.03125
- latent_from_hidden: bfloat16 [8192, 256], P('tp'), may hold values from -0.046875 to 0.046875
- key_rebuild: bfloat16 [256, 1024], replicated, may hold values from -0.375 to 0.375
- value_rebuild: bfloat16 [256, 1024], replicated, may hold values from -0.375 to 0.375
- queries: bfloat16 [8192, 8192], P('ctx', 'tp'), may hold values from -720 to 720
Outputs:
- mamba_out: bfloat16 [8192, 16384], P('ctx', 'tp')
- attended: bfloat16 [8192, 8192], P('ctx', 'tp')
The draws below stay inside these ranges and needn't reach their ends.
All inputs are finite; a program needn't handle non-finite values.
Results may differ from the reference program's by a relative error of at most 0.035.
Values may be sent and summed in bfloat16 or wider, within the bound.
No kernel may reach another device: no remote copies, remote signals or barrier semaphores. Data moves between devices by JAX's collectives and lax.ppermute only.
A program may use at most 64 MiB of HBM per device.

```python
import math
import jax
import jax.numpy as jnp
from jax import lax

D = 8192
INNER = 16384
STATE = 16
HEADDIM = 64
STRETCH = 256
HEADS = 64
KVH = 8
HD = 128
RANK = 256
PROMPT_TOKENS = 8192
MIXER_HEADS = 256
GROUP = 8


def head_rates(key, slow_share):
    kind_key, slow_key, fast_key = jax.random.split(key, 3)
    is_slow = jax.random.uniform(kind_key, (MIXER_HEADS,), jnp.float32) < slow_share
    slow_rate = jax.random.uniform(slow_key, (MIXER_HEADS,), jnp.float32, minval=0.05, maxval=0.5) / PROMPT_TOKENS
    fast_rate = jnp.exp(jax.random.uniform(fast_key, (MIXER_HEADS,), jnp.float32, minval=math.log(1.0 / 60.0), maxval=math.log(1.0 / 20.0)))
    return jnp.where(is_slow, slow_rate, fast_rate)


def draw_decay_rate(key, part):
    slow_share = 0.5
    return head_rates(key, slow_share)


def draw_step_size(key, part):
    slow_share = 0.5
    per_head_rate = head_rates(key, slow_share)
    key = jax.random.fold_in(key, 7)
    token_random_key, block_random_key, location_key, spike_random_key = jax.random.split(key, 4)
    baseline_step = jax.random.uniform(token_random_key, (MIXER_HEADS, PROMPT_TOKENS), jnp.float32, minval=0.5, maxval=1.5)
    block_scale = jnp.exp(jax.random.uniform(block_random_key, (MIXER_HEADS, PROMPT_TOKENS // 64, 1), jnp.float32, minval=math.log(0.5), maxval=math.log(2.0)))
    baseline_step = (baseline_step.reshape(MIXER_HEADS, PROMPT_TOKENS // 64, 64) * block_scale).reshape(MIXER_HEADS, PROMPT_TOKENS)
    locations = jax.random.randint(location_key, (3,), 0, PROMPT_TOKENS)
    spike_events = jnp.any(jnp.arange(PROMPT_TOKENS)[None, :] == locations[:, None], axis=0)
    quantity_total = jax.random.uniform(spike_random_key, (MIXER_HEADS, 1), jnp.float32, minval=0.22, maxval=0.45) / per_head_rate[:, None]
    return jnp.where(spike_events[None, :], quantity_total, baseline_step)


def draw_queries(key, part):
    key = jax.random.fold_in(key, 11)
    values = jnp.clip(3.0 * jax.random.normal(key, (PROMPT_TOKENS, HEADS * HD), jnp.float32), -18.0, 18.0)
    return values.astype(jnp.bfloat16)


def shard_levels(key, dims, cuts, least, high):
    def one(dim, blocks):
        heights = jax.random.uniform(jax.random.fold_in(jax.random.fold_in(key, 6), dim), (blocks,), jnp.float32, least / len(cuts), high / len(cuts))
        return jnp.repeat(jnp.exp(heights), dims[dim] // blocks).reshape((-1,) + (1,) * (len(dims) - dim - 1))

    level = one(*cuts[0])
    for cut in cuts[1:]:
        level = level * one(*cut)
    return level


def noise(key, extent, scale, bound, shards=(), kind=jnp.bfloat16):
    entries = scale * jax.random.normal(key, extent, jnp.float32)
    if shards:
        entries = entries * shard_levels(key, extent, shards, -0.22, 0.18)
    return jnp.clip(entries, -bound, bound).astype(kind)


def setup_inputs(seed: int = 0) -> dict:
    arg_keys = jax.random.split(jax.random.key(seed), 14)
    return {
        "hidden_states": noise(arg_keys[0], (PROMPT_TOKENS, D), 1.0, 6.0, ((0, 32), (1, 16))),
        "ssm_input": noise(arg_keys[1], (PROMPT_TOKENS, INNER), 1.0, 6.0, ((0, 32), (1, 16))),
        "step_size": draw_step_size(jax.random.fold_in(arg_keys[13], 71), 0),
        "decay_rate": draw_decay_rate(jax.random.fold_in(arg_keys[13], 71), 0),
        "proj_b": noise(arg_keys[4], (STATE, PROMPT_TOKENS), 0.25, 1.5, ((1, 32),)),
        "proj_c": noise(arg_keys[5], (STATE, PROMPT_TOKENS), 0.25, 1.5, ((1, 32),)),
        "skip_gain": jnp.clip(0.5 + 1.5 * jax.random.uniform(arg_keys[6], (MIXER_HEADS,), jnp.float32) ** shard_levels(arg_keys[6], (MIXER_HEADS,), ((0, 16),), -0.2, 0.2), 0.5, 2.0),
        "norm_gain": jnp.clip(1.0 + 0.1 * jax.random.normal(arg_keys[7], (INNER,), jnp.float32), 0.5, 1.5),
        "latent_from_ssm": noise(arg_keys[8], (INNER, RANK), (2 * INNER) ** -0.5, 0.03125, ((0, 16),)),
        "latent_from_hidden": noise(arg_keys[9], (D, RANK), (2 * D) ** -0.5, 0.046875, ((0, 16),)),
        "key_rebuild": noise(arg_keys[10], (RANK, KVH * HD), RANK ** -0.5, 0.375),
        "value_rebuild": noise(arg_keys[11], (RANK, KVH * HD), RANK ** -0.5, 0.375),
        "queries": draw_queries(jax.random.fold_in(arg_keys[13], 71), 0),
    }


NEG_BIG = -1e+30
EPSILON = 1e-05
HIGHEST = lax.Precision.HIGHEST

def ssm_layer(ssm_input, step_size, decay_rate, proj_b, proj_c, skip_gain, norm_gain):
    head_count = INNER // HEADDIM
    block_count = PROMPT_TOKENS // STRETCH
    log_step = -decay_rate[:, None] * step_size
    within = jnp.cumsum(log_step.reshape(head_count, block_count, STRETCH), axis=2)
    causal = jnp.arange(STRETCH)[:, None] >= jnp.arange(STRETCH)[None, :]
    x_blocks = ssm_input.reshape(block_count, STRETCH, head_count, HEADDIM)
    b_blocks = jnp.transpose(proj_b.reshape(STATE, block_count, STRETCH), (1, 0, 2))
    c_blocks = jnp.transpose(proj_c.reshape(STATE, block_count, STRETCH), (1, 0, 2))

    def advance(carried, element):
        log_within, x_block, b_block, c_block = element
        intersection = jnp.dot(c_block.T, b_block, preferred_element_type=jnp.float32)
        gaps = log_within[:, :, None] - log_within[:, None, :]
        decays = jnp.where(causal[None], jnp.exp(jnp.where(causal[None], gaps, 0.0)), 0.0)
        mixing = (intersection[None] * decays).astype(jnp.bfloat16)
        output = jnp.einsum('hts,shp->thp', mixing.astype(jnp.float32), x_block.astype(jnp.float32), precision=HIGHEST)
        from_state = jnp.einsum('nt,hpn->thp', c_block.astype(jnp.float32), carried, precision=HIGHEST)
        output = output + from_state * jnp.exp(log_within).T[:, :, None]
        to_end = jnp.exp(log_within[:, -1:] - log_within)
        weighted = x_block.astype(jnp.float32) * to_end.T[:, :, None]
        fresh_state = jnp.einsum('shp,ns->hpn', weighted, b_block.astype(jnp.float32), precision=HIGHEST)
        carried = jnp.exp(log_within[:, -1])[:, None, None] * carried + fresh_state
        return (carried, output)
    empty_state = jnp.zeros((head_count, HEADDIM, STATE), jnp.float32)
    _, outputs = lax.scan(advance, empty_state, (jnp.transpose(within, (1, 0, 2)), x_blocks, b_blocks, c_blocks))
    ssm_out = outputs + skip_gain[None, None, :, None] * x_blocks.astype(jnp.float32)
    square_mean = lax.optimization_barrier(jnp.mean(ssm_out * ssm_out, axis=-1, keepdims=True))
    normalized = ssm_out * lax.rsqrt(square_mean + EPSILON)
    return (normalized.reshape(PROMPT_TOKENS, INNER) * norm_gain[None, :]).astype(jnp.bfloat16)

def attention(latents, key_rebuild, value_rebuild, queries):
    key_rows = jnp.dot(latents, key_rebuild, preferred_element_type=jnp.float32).astype(jnp.bfloat16)
    value_rows = jnp.dot(latents, value_rebuild, preferred_element_type=jnp.float32).astype(jnp.bfloat16)
    block_size = math.gcd(PROMPT_TOKENS, 512)
    block_count = PROMPT_TOKENS // block_size
    key_blocks = key_rows.reshape(block_count, block_size, KVH, HD)
    value_blocks = value_rows.reshape(block_count, block_size, KVH, HD)
    grouped = queries.reshape(block_count, block_size, KVH, GROUP, HD)
    scale = 1.0 / math.sqrt(HD)
    offsets = jnp.arange(block_size, dtype=jnp.int32)

    def one_query_block(query_index):
        query_rows = lax.dynamic_index_in_dim(grouped, query_index, 0, keepdims=False).astype(jnp.float32)
        query_pos = query_index * block_size + offsets

        def visit(carried, key_index):

            def work(running):
                best, norm_sum, accum = running
                key_blk = lax.dynamic_index_in_dim(key_blocks, key_index, 0, keepdims=False).astype(jnp.float32)
                value_blk = lax.dynamic_index_in_dim(value_blocks, key_index, 0, keepdims=False).astype(jnp.float32)
                scores = jnp.einsum('tkgd,skd->kgts', query_rows, key_blk, precision=HIGHEST) * scale
                allowed = (key_index * block_size + offsets)[None, :] <= query_pos[:, None]
                scores = jnp.where(allowed, scores, -jnp.inf)
                new_best = jnp.maximum(best, lax.optimization_barrier(jnp.max(scores, axis=-1)))
                factor = jnp.exp(best - new_best)
                weights = jnp.exp(scores - new_best[..., None])
                norm_sum = norm_sum * factor + lax.optimization_barrier(jnp.sum(weights, axis=-1))
                rounded = lax.optimization_barrier(weights.astype(jnp.bfloat16)).astype(jnp.float32)
                accum = accum * factor[..., None] + jnp.einsum('kgts,skd->kgtd', rounded, value_blk, precision=HIGHEST)
                return (new_best, norm_sum, accum)
            needed = key_index * block_size <= query_index * block_size + block_size - 1
            return (lax.cond(needed, work, lambda unchanged: unchanged, carried), None)
        starting = (jnp.full((KVH, GROUP, block_size), NEG_BIG, jnp.float32), jnp.zeros((KVH, GROUP, block_size), jnp.float32), jnp.zeros((KVH, GROUP, block_size, HD), jnp.float32))
        finished, _ = lax.scan(visit, starting, jnp.arange(block_count, dtype=jnp.int32))
        result = finished[2] / finished[1][..., None]
        result = jnp.transpose(result, (2, 0, 1, 3)).reshape(block_size, HEADS * HD)
        return result.astype(jnp.bfloat16)
    pieces = lax.map(one_query_block, jnp.arange(block_count, dtype=jnp.int32))
    return pieces.reshape(PROMPT_TOKENS, HEADS * HD)

def reference(hidden_states, ssm_input, step_size, decay_rate, proj_b, proj_c, skip_gain, norm_gain, latent_from_ssm, latent_from_hidden, key_rebuild, value_rebuild, queries):
    mamba_out = ssm_layer(ssm_input, step_size, decay_rate, proj_b, proj_c, skip_gain, norm_gain)
    latent_terms = jnp.dot(mamba_out, latent_from_ssm, preferred_element_type=jnp.float32)
    latent_terms = latent_terms + jnp.dot(hidden_states, latent_from_hidden, preferred_element_type=jnp.float32)
    latents = latent_terms.astype(jnp.bfloat16)
    attended = attention(latents, key_rebuild, value_rebuild, queries)
    return (mamba_out, attended)
```

```python
import functools
import math

import jax
import jax.numpy as jnp
from jax import lax
from jax.experimental import pallas as pl
from jax.experimental.pallas import tpu as pltpu
from jax.sharding import Mesh
from jax.sharding import PartitionSpec as P

STATE = 16
HEADDIM = 64
ROWS = 256
HEADS_SSM = 16
INNER = HEADS_SSM * HEADDIM
HD = 128
RANK = 256
HEADS_Q = 4
NY, NX, NZ, NC = 8, 4, 8, 2
NT = NZ * NC
PIECE = ROWS // NT
HALF = ROWS // NC
NCTX = NY * NX
PAY = INNER + 128
BLOCKS = INNER // 128

NEG_BIG = -1e30
EPSILON = 1e-05
SCALE2 = math.log2(math.e) / math.sqrt(HD)
F32 = jnp.float32
BF16 = jnp.bfloat16
MIB = 1 << 20

VM = pl.BlockSpec(memory_space=pltpu.VMEM)
ANY = pl.BlockSpec(memory_space=pl.ANY)
SM = pl.BlockSpec(memory_space=pltpu.SMEM)


def iota(shape, axis):
    return lax.broadcasted_iota(jnp.int32, shape, axis)


def dot(a, b):
    return jnp.dot(a, b, preferred_element_type=F32)


def split(value):
    high = value.astype(BF16)
    return high, (value - high.astype(F32)).astype(BF16)


def spread():
    lane = iota((128, INNER), 0)
    head = iota((128, INNER), 1) // HEADDIM
    return jnp.where((lane < 2 * HEADS_SSM) & ((lane & 15) == head), 1.0, 0.0).astype(BF16)


def within_rows(step_ref, rate_ref):
    row = iota((HEADS_SSM, ROWS), 0)
    lane = iota((HEADS_SSM, ROWS), 1)
    rate = jnp.zeros((HEADS_SSM, ROWS), F32)
    for h in range(HEADS_SSM):
        rate = jnp.where(row == h, rate_ref[h], rate)
    total = -rate * step_ref[...]
    shift = 1
    while shift < ROWS:
        total = total + jnp.where(lane >= shift, pltpu.roll(total, shift, 1), 0.0)
        shift *= 2
    return total


def pack_decay(compact):
    lane = iota(compact.shape, 1)
    kept = jnp.where(lane < HEADS_SSM, compact, 0.0)
    high = kept.astype(BF16).astype(F32)
    low = pltpu.roll(kept - high, HEADS_SSM, 1)
    return (high + low).astype(BF16)


def unpack_decay(packed):
    value = packed.astype(F32)
    lane = iota(value.shape, 1)
    return jnp.where(lane < HEADS_SSM, value + pltpu.roll(value, 128 - HEADS_SSM, 1), 0.0)


def state_kernel(rate_ref, x_ref, step_ref, b_ref, pay_ref):
    within = within_rows(step_ref, rate_ref)
    last = within[:, ROWS - 1 : ROWS]
    to_end = jnp.exp(last - within)
    b = b_ref[...].astype(F32)
    lane = iota((STATE, 128), 1)
    for j in range(BLOCKS):
        cols = slice(128 * j, 128 * (j + 1))
        a0h, a0l = split(to_end[2 * j : 2 * j + 1, :] * b)
        a1h, a1l = split(to_end[2 * j + 1 : 2 * j + 2, :] * b)
        lhs = jnp.concatenate([a0h, a1h, a0l, a1l], axis=0)
        out = dot(lhs, x_ref[:, cols])
        both = out[: 2 * STATE] + out[2 * STATE :]
        state = jnp.where(lane < HEADDIM, both[:STATE], both[STATE:])
        for i in range(NX):
            pay_ref[i, :, cols] = state.astype(BF16)
    head = iota((HEADS_SSM, 128), 0)
    hlane = iota((HEADS_SSM, 128), 1)
    compact = jnp.sum(jnp.where(hlane == head, jnp.exp(last), 0.0), axis=0, keepdims=True)
    packed = pack_decay(jnp.broadcast_to(compact, (STATE, 128)))
    for i in range(NX):
        pay_ref[i, :, INNER:] = packed


def widened(spans_ref, count):
    packed = jnp.concatenate([spans_ref[i, :, INNER:] for i in range(count)], axis=0)
    wide = dot(packed, spread())
    return [wide[i * STATE : (i + 1) * STATE] for i in range(count)]


def row_kernel(place_ref, spans_ref, total_ref, before_ref, decay_ref):
    x = place_ref[1]
    wide = widened(spans_ref, NX)
    run = jnp.zeros((STATE, INNER), F32)
    before = run
    before_decay = jnp.ones((STATE, INNER), F32)
    compact = jnp.ones((STATE, 128), F32)
    for i in range(NX):
        run = wide[i] * run + spans_ref[i, :, :INNER].astype(F32)
        before = jnp.where(i < x, run, before)
        before_decay = jnp.where(i < x, wide[i] * before_decay, before_decay)
        compact = compact * unpack_decay(spans_ref[i, :, INNER:])
    before_ref[...] = before
    decay_ref[...] = before_decay
    total = run.astype(BF16)
    packed = pack_decay(compact)
    for i in range(NY):
        total_ref[i, :, :INNER] = total
        total_ref[i, :, INNER:] = packed


def intra_kernel(
    rate_ref, skip_ref, x_ref, step_ref, b_ref, c_ref, y_ref, grow_ref
):
    within = within_rows(step_ref, rate_ref)
    columns = jnp.concatenate([within, jnp.zeros((128 - HEADS_SSM, ROWS), F32)], axis=0).T
    grow = jnp.exp(columns)
    grow_ref[...] = pack_decay(grow)
    meet = lax.dot_general(
        c_ref[...], b_ref[...], (((0,), (0,)), ((), ())), preferred_element_type=F32
    )
    half = ROWS // 2
    causal = iota((half, half), 0) >= iota((half, half), 1)
    lane = iota((ROWS, 128), 1)
    zeros = jnp.zeros((half, half), BF16)

    def mixing(h):
        row = within[h : h + 1, :]
        column = columns[:, h : h + 1]
        top, bottom = column[:half], column[half:]
        left, right = row[:, :half], row[:, half:]
        m00 = meet[:half, :half] * jnp.exp(jnp.where(causal, top - left, NEG_BIG))
        m10 = meet[half:, :half] * jnp.exp(bottom - left)
        m11 = meet[half:, half:] * jnp.exp(jnp.where(causal, bottom - right, NEG_BIG))
        upper = jnp.concatenate([m00.astype(BF16), zeros], axis=1)
        lower = jnp.concatenate([m10.astype(BF16), m11.astype(BF16)], axis=1)
        return jnp.concatenate([upper, lower], axis=0)

    for j in range(HEADS_SSM // 2):
        cols = slice(128 * j, 128 * (j + 1))
        x = x_ref[:, cols]
        out0 = dot(mixing(2 * j), x)
        out1 = dot(mixing(2 * j + 1), x)
        skip = jnp.where(lane < HEADDIM, skip_ref[2 * j], skip_ref[2 * j + 1])
        y_ref[:, cols] = jnp.where(lane < HEADDIM, out0, out1) + skip * x.astype(F32)


def finish_kernel(
    place_ref, rows_ref, before_ref, decay_ref, y_ref, grow_ref, c_ref, gain_ref, w_ref, h_ref,
    mamba_ref, part_ref,
):
    chan = spread()
    wide = widened(rows_ref, NY - 1)
    run = jnp.zeros((STATE, INNER), F32)
    for row in range(NY - 1):
        joined = wide[row] * run + rows_ref[row, :, :INNER].astype(F32)
        run = jnp.where(row < place_ref[0], joined, run)
    carried = run * decay_ref[...] + before_ref[...]
    high, low = split(carried)
    c = c_ref[...]
    from_state = lax.dot_general(
        jnp.concatenate([c, c], axis=0),
        jnp.concatenate([high, low], axis=0),
        (((0,), (0,)), ((), ())),
        preferred_element_type=F32,
    )
    grow = dot(grow_ref[...], chan)
    out = y_ref[...] + from_state * grow
    gather = jnp.where(
        iota((INNER, 128), 0) // HEADDIM == iota((INNER, 128), 1), 1.0, 0.0
    ).astype(BF16)
    square = dot((out * out).astype(BF16), gather) * (1.0 / HEADDIM)
    inverse = dot(pack_decay(lax.rsqrt(square + EPSILON)), chan)
    mamba = (out * inverse * gain_ref[...]).astype(BF16)
    mamba_ref[...] = mamba
    part_ref[...] = (dot(mamba, w_ref[...]) + h_ref[...]).astype(BF16)


def copy_kernel(q_ref, out_ref):
    out_ref[...] = q_ref[...]


def sum_kernel(pieces_ref, out_ref):
    total = pieces_ref[0].astype(F32)
    for i in range(1, NT):
        total = total + pieces_ref[i].astype(F32)
    rounded = total.astype(BF16)
    for i in range(NY * NZ):
        out_ref[i] = rounded


def hidden_kernel(hidden_ref, w_ref, out_ref):
    out_ref[...] = dot(hidden_ref[...], w_ref[...])


def weights_kernel(place_ref, wk_ref, wv_ref, order_ref, out_ref):
    out_ref[:, :HD] = wk_ref[...]
    out_ref[:, HD:] = wv_ref[...]


def rebuild_kernel(place_ref, mine_ref, w_ref, out_ref):
    y = place_ref[0]
    w = w_ref[...]
    for block in range(NY):
        begin = ((y - block) & (NY - 1)) * HALF
        out = pl.ds(pl.multiple_of(begin, HALF), HALF)
        rows = dot(mine_ref[block], w)
        out_ref[out, :HD] = (rows[:, :HD] * SCALE2).astype(BF16)
        out_ref[out, HD:] = rows[:, HD:].astype(BF16)


def place_keys(y, mine_ref, other_ref, k_ref, v_ref):
    lane = iota((HALF, HD), 1)
    ones = jnp.ones((HALF, HD), BF16)
    for part, ref in enumerate((mine_ref, other_ref)):
        for block in range(NY):
            rows = slice(block * HALF, (block + 1) * HALF)
            out = slice((part * NY + block) * HALF, (part * NY + block + 1) * HALF)
            bias = jnp.where(y >= block, 0.0, NEG_BIG)
            k_ref[out, :HD] = ref[rows, :HD]
            k_ref[out, HD:] = jnp.where(lane == 0, bias, 0.0).astype(BF16)
            v_ref[out, :HD] = ref[rows, HD:]
            v_ref[out, HD:] = ones


def attend_kernel(step, place_ref, q_ref, k_ref, v_ref, out_ref):
    x, core = place_ref[1], place_ref[3]
    ahead = ((x ^ step) - x) * ROWS
    lane = iota((ROWS, 128), 1)
    unit = jnp.where(lane == 0, 1.0, 0.0).astype(BF16)
    token = iota((ROWS, HALF), 0) + ahead
    slot = iota((ROWS, HALF), 1)
    allowed = []
    for own in (core, 1 - core):
        key = (slot // PIECE) * (2 * PIECE) + own * PIECE + (slot & (PIECE - 1))
        allowed.append(key <= token)

    allowed = [jnp.concatenate([part, part], axis=0) for part in allowed]

    def scored(first, part):
        query = jnp.concatenate(
            [
                jnp.concatenate([q_ref[:, h * HD : (h + 1) * HD], unit], axis=1)
                for h in (first, first + 1)
            ],
            axis=0,
        )
        scores = lax.dot_general(
            query,
            k_ref[part * NY * HALF : (part + 1) * NY * HALF, :],
            (((1,), (1,)), ((), ())),
            preferred_element_type=F32,
        )
        near = jnp.where(allowed[part], scores[:, :HALF], NEG_BIG)
        return jnp.concatenate([near, scores[:, HALF:]], axis=1)

    stats = jnp.zeros((ROWS, 128), F32)
    following = scored(0, 0)
    for first in range(0, HEADS_Q, 2):
        best = sums = None
        for part in range(2):
            scores = following
            if part == 0:
                following = scored(first, 1)
            elif first + 2 < HEADS_Q:
                following = scored(first + 2, 0)
            chunk_best = jnp.max(scores, axis=1, keepdims=True)
            values = v_ref[part * NY * HALF : (part + 1) * NY * HALF, :]
            if part == 0:
                best = chunk_best
                sums = dot(jnp.exp2(scores - best).astype(BF16), values)
            else:
                old, best = best, jnp.maximum(best, chunk_best)
                sums = sums * jnp.exp2(old - best) + dot(
                    jnp.exp2(scores - best).astype(BF16), values
                )
        norm = sums[:, HD:]
        ratio = (sums[:, :HD] / norm).astype(BF16)
        level = best + jnp.log2(norm)
        for h in (first, first + 1):
            rows = slice((h - first) * ROWS, (h - first + 1) * ROWS)
            out_ref[:ROWS, h * HD : (h + 1) * HD] = ratio[rows]
            stats = jnp.where(lane == h, level[rows], stats)
    rows = stats.T[:8, :]
    high, mid = split(rows)
    low = (rows - high.astype(F32) - mid.astype(F32)).astype(BF16)
    upper = jnp.concatenate([high, mid], axis=1)
    lower = jnp.concatenate([low, jnp.zeros((8, ROWS), BF16)], axis=1)
    out_ref[ROWS:, :] = jnp.concatenate([upper, lower], axis=0)


def attend_first_kernel(step, place_ref, q_ref, mine_ref, other_ref, out_ref, k_ref, v_ref):
    place_keys(place_ref[0], mine_ref, other_ref, k_ref, v_ref)
    attend_kernel(step, place_ref, q_ref, k_ref, v_ref, out_ref)


def combine_kernel(own_ref, back1_ref, back2_ref, back3_ref, out_ref):
    refs = [own_ref, back1_ref, back2_ref, back3_ref]
    logs = []
    for ref in refs:
        tail = ref[ROWS:, :].astype(F32)
        logs.append(tail[:8, :ROWS] + tail[:8, ROWS:] + tail[8:, :ROWS])
    best = jnp.maximum(jnp.maximum(logs[0], logs[1]), jnp.maximum(logs[2], logs[3]))
    shares = [jnp.exp2(log - best) for log in logs]
    inverse = 1.0 / (shares[0] + shares[1] + shares[2] + shares[3])
    table = jnp.concatenate(
        [share * inverse for share in shares] + [jnp.zeros((128 - 32, ROWS), F32)], axis=0
    ).T
    for h in range(HEADS_Q):
        cols = slice(h * HD, (h + 1) * HD)
        total = jnp.zeros((ROWS, HD), F32)
        for i, ref in enumerate(refs):
            total += table[:, 8 * i + h : 8 * i + h + 1] * ref[:ROWS, cols].astype(F32)
        out_ref[:, cols] = total.astype(BF16)


def call(kernel, name, out_shape, in_specs, limit, flops, moved, streamed=False, **options):
    out_specs = jax.tree.map(lambda _: VM, out_shape)
    if streamed:
        options["grid"] = (1,)
        in_specs = [
            spec if spec in (SM, ANY) else pl.BlockSpec(spec, lambda i, n=len(spec): (0,) * n)
            for spec in in_specs
        ]
        out_specs = jax.tree.map(
            lambda out: pl.BlockSpec(out.shape, lambda i, n=len(out.shape): (0,) * n), out_shape
        )
    return pl.pallas_call(
        kernel,
        out_shape=out_shape,
        in_specs=in_specs,
        out_specs=out_specs,
        name=name,
        cost_estimate=pl.CostEstimate(flops=flops, bytes_accessed=moved, transcendentals=0),
        compiler_params=pltpu.CompilerParams(vmem_limit_bytes=limit * MIB),
        **options,
    )


def shape(dims, kind):
    return jax.ShapeDtypeStruct(dims, kind)


def swap(value, axis, size, step):
    return lax.ppermute(value, axis, [(i, i ^ step) for i in range(size)])


def exchange(chunks, axes):
    return lax.all_to_all(chunks, axes, 0, 0, tiled=True)


def after(kernel, inputs):
    def ordered(*refs):
        kernel(*refs[:inputs], *refs[inputs + 1 :])

    return ordered


def body(
    hidden_states,
    ssm_input,
    step_size,
    decay_rate,
    proj_b,
    proj_c,
    skip_gain,
    norm_gain,
    latent_from_ssm,
    latent_from_hidden,
    key_rebuild,
    value_rebuild,
    queries,
):
    place = jnp.stack(
        [lax.axis_index(axis) for axis in ("y", "x", "z", "core")]
    ).astype(jnp.int32)

    payload = call(
        state_kernel,
        "state",
        shape((NX, STATE, PAY), BF16),
        [SM, (ROWS, INNER), (HEADS_SSM, ROWS), (STATE, ROWS)],
        60,
        1 << 27,
        MIB,
        streamed=True,
    )(decay_rate, ssm_input, step_size, proj_b)
    spans = exchange(payload, "x")
    from_hidden = call(
        after(hidden_kernel, 2),
        "hidden",
        shape((ROWS, RANK), F32),
        [VM, VM, ANY],
        16,
        1 << 31,
        MIB,
    )(hidden_states, latent_from_hidden, payload)
    totals, before, row_decay = call(
        after(row_kernel, 2),
        "row",
        (
            shape((NY, STATE, PAY), BF16),
            shape((STATE, INNER), F32),
            shape((STATE, INNER), F32),
        ),
        [SM, VM, ANY],
        8,
        1 << 24,
        MIB // 2,
    )(place, spans, from_hidden)

    rows = exchange(totals, "y")
    partial, growth = call(
        after(intra_kernel, 6),
        "intra",
        (shape((ROWS, INNER), F32), shape((ROWS, 128), BF16)),
        [SM, SM] + [VM] * 4 + [ANY],
        24,
        1 << 31,
        3 * MIB,
    )(decay_rate, skip_gain, ssm_input, step_size, proj_b, proj_c, before)
    mamba_out, latent_terms = call(
        finish_kernel,
        "finish",
        (shape((ROWS, INNER), BF16), shape((ROWS, RANK), BF16)),
        [SM] + [VM] * 9,
        24,
        1 << 29,
        4 * MIB,
    )(
        place, rows, before, row_decay, partial, growth, proj_c, norm_gain.reshape(1, INNER),
        latent_from_ssm, from_hidden,
    )

    def copied(done):
        return call(
            after(copy_kernel, 1), "copy", shape(queries.shape, BF16), [VM, ANY], 8, 1 << 27, MIB
        )(queries, done)

    pieces = exchange(latent_terms.reshape(NT, PIECE, RANK), ("z", "core"))
    lent = copied(latent_terms)
    latents = call(
        after(sum_kernel, 1),
        "sum",
        shape((NY * NZ, PIECE, RANK), BF16),
        [VM, ANY],
        8,
        1 << 20,
        MIB // 2,
    )(pieces, lent)

    blocks = exchange(latents, ("y", "z")).reshape(NY, HALF, RANK)
    lent = copied(latents)
    visiting1, visiting2, visiting3 = [swap(lent, "x", NX, k) for k in (1, 2, 3)]
    weights = pl.pallas_call(
        weights_kernel,
        out_shape=shape((RANK, 2 * HD), BF16),
        grid_spec=pltpu.PrefetchScalarGridSpec(
            num_scalar_prefetch=1,
            grid=(1,),
            in_specs=[pl.BlockSpec((RANK, HD), lambda i, place: (0, place[2]))] * 2 + [ANY],
            out_specs=pl.BlockSpec((RANK, 2 * HD), lambda i, place: (0, 0)),
        ),
        name="weights",
        cost_estimate=pl.CostEstimate(flops=1 << 30, bytes_accessed=MIB, transcendentals=0),
        compiler_params=pltpu.CompilerParams(vmem_limit_bytes=8 * MIB),
    )(place, key_rebuild, value_rebuild, latents)
    mine = call(
        after(after(after(rebuild_kernel, 3), 3), 3),
        "rebuild",
        shape((NY * HALF, 2 * HD), BF16),
        [SM, VM, VM, ANY, ANY, ANY],
        8,
        1 << 27,
        MIB,
    )(place, blocks, weights, visiting1, visiting2, visiting3)
    other = swap(mine, "core", NC, 1)

    work = 4 * ROWS * HEADS_Q * HD * NY * ROWS
    answer = shape((ROWS + 16, HEADS_Q * HD), BF16)
    wide = shape((NY * ROWS, 2 * HD), BF16)
    done, keys, values = call(
        functools.partial(attend_first_kernel, 2), "attend", (answer, wide, wide),
        [SM, VM, VM, VM], 24, work, 4 * MIB,
    )(place, visiting2, mine, other)
    back = {2: swap(done, "x", NX, 2)}
    for step, query, awaited in ((1, visiting1, None), (3, visiting3, None), (0, queries, 2)):
        kernel = functools.partial(attend_kernel, step)
        operands = [place, query, keys, values, done]
        if awaited is not None:
            operands.append(back[awaited])
            kernel = after(kernel, 4)
        done = call(
            after(kernel, 4), "attend", answer, [SM, VM, VM, VM] + [ANY] * (len(operands) - 4),
            24, work, 4 * MIB,
        )(*operands)
        if step:
            back[step] = swap(done, "x", NX, step)

    attended = call(
        combine_kernel,
        "combine",
        shape((ROWS, HEADS_Q * HD), BF16),
        [VM] * 4,
        16,
        1 << 20,
        2 * MIB,
    )(done, back[1], back[2], back[3])
    return (mamba_out, attended)


def solution(mesh):
    grid = Mesh(mesh.devices.reshape(NY, NX, NZ, NC), ("y", "x", "z", "core"))
    ctx, tp = ("y", "x"), ("z", "core")
    return jax.shard_map(
        body,
        mesh=grid,
        in_specs=(
            P(ctx, tp),
            P(ctx, tp),
            P(tp, ctx),
            P(tp),
            P(None, ctx),
            P(None, ctx),
            P(tp),
            P(tp),
            P(tp, None),
            P(tp, None),
            P(),
            P(),
            P(ctx, tp),
        ),
        out_specs=(P(ctx, tp), P(ctx, tp)),
        check_vma=False,
    )
```

```python
import functools
import math

import jax
import jax.numpy as jnp
from jax import lax
from jax.experimental import pallas as pl
from jax.experimental.pallas import tpu as pltpu
from jax.sharding import Mesh
from jax.sharding import PartitionSpec as P

STATE = 16
HEADDIM = 64
ROWS = 256
HEADS_SSM = 16
INNER = HEADS_SSM * HEADDIM
HD = 128
RANK = 256
HEADS_Q = 4
NY, NX, NZ, NC = 8, 4, 8, 2
NT = NZ * NC
PIECE = ROWS // NT
HALF = ROWS // NC
NCTX = NY * NX
PAY = INNER + 128
BLOCKS = INNER // 128

NEG_BIG = -1e30
EPSILON = 1e-05
SCALE2 = math.log2(math.e) / math.sqrt(HD)
F32 = jnp.float32
BF16 = jnp.bfloat16
MIB = 1 << 20

VM = pl.BlockSpec(memory_space=pltpu.VMEM)
ANY = pl.BlockSpec(memory_space=pl.ANY)
SM = pl.BlockSpec(memory_space=pltpu.SMEM)


def iota(shape, axis):
    return lax.broadcasted_iota(jnp.int32, shape, axis)


def dot(a, b):
    return jnp.dot(a, b, preferred_element_type=F32)


def split(value):
    high = value.astype(BF16)
    return high, (value - high.astype(F32)).astype(BF16)


def spread():
    lane = iota((128, INNER), 0)
    head = iota((128, INNER), 1) // HEADDIM
    return jnp.where((lane < 2 * HEADS_SSM) & ((lane & 15) == head), 1.0, 0.0).astype(BF16)


def within_rows(step_ref, rate_ref):
    row = iota((HEADS_SSM, ROWS), 0)
    lane = iota((HEADS_SSM, ROWS), 1)
    rate = jnp.zeros((HEADS_SSM, ROWS), F32)
    for h in range(HEADS_SSM):
        rate = jnp.where(row == h, rate_ref[h], rate)
    total = -rate * step_ref[...]
    shift = 1
    while shift < ROWS:
        total = total + jnp.where(lane >= shift, pltpu.roll(total, shift, 1), 0.0)
        shift *= 2
    return total


def pack_decay(compact):
    lane = iota(compact.shape, 1)
    kept = jnp.where(lane < HEADS_SSM, compact, 0.0)
    high = kept.astype(BF16).astype(F32)
    low = pltpu.roll(kept - high, HEADS_SSM, 1)
    return (high + low).astype(BF16)


def unpack_decay(packed):
    value = packed.astype(F32)
    lane = iota(value.shape, 1)
    return jnp.where(lane < HEADS_SSM, value + pltpu.roll(value, 128 - HEADS_SSM, 1), 0.0)


def state_kernel(rate_ref, x_ref, step_ref, b_ref, pay_ref):
    within = within_rows(step_ref, rate_ref)
    last = within[:, ROWS - 1 : ROWS]
    to_end = jnp.exp(last - within)
    b = b_ref[...].astype(F32)
    lane = iota((STATE, 128), 1)
    for j in range(BLOCKS):
        cols = slice(128 * j, 128 * (j + 1))
        a0h, a0l = split(to_end[2 * j : 2 * j + 1, :] * b)
        a1h, a1l = split(to_end[2 * j + 1 : 2 * j + 2, :] * b)
        lhs = jnp.concatenate([a0h, a1h, a0l, a1l], axis=0)
        out = dot(lhs, x_ref[:, cols])
        both = out[: 2 * STATE] + out[2 * STATE :]
        state = jnp.where(lane < HEADDIM, both[:STATE], both[STATE:])
        for i in range(NX):
            pay_ref[i, :, cols] = state.astype(BF16)
    head = iota((HEADS_SSM, 128), 0)
    hlane = iota((HEADS_SSM, 128), 1)
    compact = jnp.sum(jnp.where(hlane == head, jnp.exp(last), 0.0), axis=0, keepdims=True)
    packed = pack_decay(jnp.broadcast_to(compact, (STATE, 128)))
    for i in range(NX):
        pay_ref[i, :, INNER:] = packed


def widened(spans_ref, count):
    packed = jnp.concatenate([spans_ref[i, :, INNER:] for i in range(count)], axis=0)
    wide = dot(packed, spread())
    return [wide[i * STATE : (i + 1) * STATE] for i in range(count)]


def row_kernel(place_ref, spans_ref, total_ref, before_ref, decay_ref):
    x = place_ref[1]
    wide = widened(spans_ref, NX)
    run = jnp.zeros((STATE, INNER), F32)
    before = run
    before_decay = jnp.ones((STATE, INNER), F32)
    compact = jnp.ones((STATE, 128), F32)
    for i in range(NX):
        run = wide[i] * run + spans_ref[i, :, :INNER].astype(F32)
        before = jnp.where(i < x, run, before)
        before_decay = jnp.where(i < x, wide[i] * before_decay, before_decay)
        compact = compact * unpack_decay(spans_ref[i, :, INNER:])
    before_ref[...] = before
    decay_ref[...] = before_decay
    total = run.astype(BF16)
    packed = pack_decay(compact)
    for i in range(NY):
        total_ref[i, :, :INNER] = total
        total_ref[i, :, INNER:] = packed


def intra_kernel(
    rate_ref, skip_ref, x_ref, step_ref, b_ref, c_ref, y_ref, grow_ref
):
    within = within_rows(step_ref, rate_ref)
    columns = jnp.concatenate([within, jnp.zeros((128 - HEADS_SSM, ROWS), F32)], axis=0).T
    grow = jnp.exp(columns)
    grow_ref[...] = pack_decay(grow)
    meet = lax.dot_general(
        c_ref[...], b_ref[...], (((0,), (0,)), ((), ())), preferred_element_type=F32
    )
    half = ROWS // 2
    causal = iota((half, half), 0) >= iota((half, half), 1)
    lane = iota((ROWS, 128), 1)
    zeros = jnp.zeros((half, half), BF16)

    def mixing(h):
        row = within[h : h + 1, :]
        column = columns[:, h : h + 1]
        top, bottom = column[:half], column[half:]
        left, right = row[:, :half], row[:, half:]
        m00 = meet[:half, :half] * jnp.exp(jnp.where(causal, top - left, NEG_BIG))
        m10 = meet[half:, :half] * jnp.exp(bottom - left)
        m11 = meet[half:, half:] * jnp.exp(jnp.where(causal, bottom - right, NEG_BIG))
        upper = jnp.concatenate([m00.astype(BF16), zeros], axis=1)
        lower = jnp.concatenate([m10.astype(BF16), m11.astype(BF16)], axis=1)
        return jnp.concatenate([upper, lower], axis=0)

    for j in range(HEADS_SSM // 2):
        cols = slice(128 * j, 128 * (j + 1))
        x = x_ref[:, cols]
        out0 = dot(mixing(2 * j), x)
        out1 = dot(mixing(2 * j + 1), x)
        skip = jnp.where(lane < HEADDIM, skip_ref[2 * j], skip_ref[2 * j + 1])
        y_ref[:, cols] = jnp.where(lane < HEADDIM, out0, out1) + skip * x.astype(F32)


def finish_kernel(
    place_ref, rows_ref, before_ref, decay_ref, y_ref, grow_ref, c_ref, gain_ref, w_ref, h_ref,
    mamba_ref, part_ref,
):
    chan = spread()
    wide = widened(rows_ref, NY - 1)
    run = jnp.zeros((STATE, INNER), F32)
    for row in range(NY - 1):
        joined = wide[row] * run + rows_ref[row, :, :INNER].astype(F32)
        run = jnp.where(row < place_ref[0], joined, run)
    carried = run * decay_ref[...] + before_ref[...]
    high, low = split(carried)
    c = c_ref[...]
    from_state = lax.dot_general(
        jnp.concatenate([c, c], axis=0),
        jnp.concatenate([high, low], axis=0),
        (((0,), (0,)), ((), ())),
        preferred_element_type=F32,
    )
    grow = dot(grow_ref[...], chan)
    out = y_ref[...] + from_state * grow
    gather = jnp.where(
        iota((INNER, 128), 0) // HEADDIM == iota((INNER, 128), 1), 1.0, 0.0
    ).astype(BF16)
    square = dot((out * out).astype(BF16), gather) * (1.0 / HEADDIM)
    inverse = dot(pack_decay(lax.rsqrt(square + EPSILON)), chan)
    mamba = (out * inverse * gain_ref[...]).astype(BF16)
    mamba_ref[...] = mamba
    part_ref[...] = (dot(mamba, w_ref[...]) + h_ref[...]).astype(BF16)


def copy_kernel(q_ref, out_ref):
    out_ref[...] = q_ref[...]


def sum_kernel(pieces_ref, out_ref):
    total = pieces_ref[0].astype(F32)
    for i in range(1, NT):
        total = total + pieces_ref[i].astype(F32)
    rounded = total.astype(BF16)
    for i in range(NY * NZ):
        out_ref[i] = rounded


def hidden_kernel(hidden_ref, w_ref, out_ref):
    out_ref[...] = dot(hidden_ref[...], w_ref[...])


def weights_kernel(place_ref, wk_ref, wv_ref, order_ref, out_ref):
    out_ref[:, :HD] = wk_ref[...]
    out_ref[:, HD:] = wv_ref[...]


def rebuild_kernel(place_ref, mine_ref, w_ref, out_ref):
    y = place_ref[0]
    w = w_ref[...]
    for block in range(NY):
        begin = ((y - block) & (NY - 1)) * HALF
        out = pl.ds(pl.multiple_of(begin, HALF), HALF)
        rows = dot(mine_ref[block], w)
        out_ref[out, :HD] = (rows[:, :HD] * SCALE2).astype(BF16)
        out_ref[out, HD:] = rows[:, HD:].astype(BF16)


def place_keys(y, mine_ref, other_ref, k_ref, v_ref):
    lane = iota((HALF, HD), 1)
    ones = jnp.ones((HALF, HD), BF16)
    for part, ref in enumerate((mine_ref, other_ref)):
        for block in range(NY):
            rows = slice(block * HALF, (block + 1) * HALF)
            out = slice((part * NY + block) * HALF, (part * NY + block + 1) * HALF)
            bias = jnp.where(y >= block, 0.0, NEG_BIG)
            k_ref[out, :HD] = ref[rows, :HD]
            k_ref[out, HD:] = jnp.where(lane == 0, bias, 0.0).astype(BF16)
            v_ref[out, :HD] = ref[rows, HD:]
            v_ref[out, HD:] = ones


def attend_kernel(step, place_ref, q_ref, k_ref, v_ref, out_ref):
    x, core = place_ref[1], place_ref[3]
    ahead = ((x ^ step) - x) * ROWS
    lane = iota((ROWS, 128), 1)
    unit = jnp.where(lane == 0, 1.0, 0.0).astype(BF16)
    token = iota((ROWS, HALF), 0) + ahead
    slot = iota((ROWS, HALF), 1)
    allowed = []
    for own in (core, 1 - core):
        key = (slot // PIECE) * (2 * PIECE) + own * PIECE + (slot & (PIECE - 1))
        allowed.append(key <= token)

    def scored(first):
        query = jnp.concatenate(
            [
                jnp.concatenate([q_ref[:, h * HD : (h + 1) * HD], unit], axis=1)
                for h in (first, first + 1)
            ],
            axis=0,
        )
        return lax.dot_general(
            query, k_ref[...], (((1,), (1,)), ((), ())), preferred_element_type=F32
        )

    allowed = [jnp.concatenate([part, part], axis=0) for part in allowed]
    stats = jnp.zeros((ROWS, 128), F32)
    following = scored(0)
    for first in range(0, HEADS_Q, 2):
        scores = following
        if first + 2 < HEADS_Q:
            following = scored(first + 2)
        pieces = []
        for part in range(2):
            begin = part * NY * HALF
            pieces.append(jnp.where(allowed[part], scores[:, begin : begin + HALF], NEG_BIG))
            pieces.append(scores[:, begin + HALF : begin + NY * HALF])
        scores = jnp.concatenate(pieces, axis=1)
        best = jnp.max(scores, axis=1, keepdims=True)
        weights = jnp.exp2(scores - best).astype(BF16)
        sums = dot(weights, v_ref[...])
        norm = sums[:, HD:]
        ratio = (sums[:, :HD] / norm).astype(BF16)
        level = best + jnp.log2(norm)
        for h in (first, first + 1):
            rows = slice((h - first) * ROWS, (h - first + 1) * ROWS)
            out_ref[:ROWS, h * HD : (h + 1) * HD] = ratio[rows]
            stats = jnp.where(lane == h, level[rows], stats)
    rows = stats.T[:8, :]
    high, mid = split(rows)
    low = (rows - high.astype(F32) - mid.astype(F32)).astype(BF16)
    upper = jnp.concatenate([high, mid], axis=1)
    lower = jnp.concatenate([low, jnp.zeros((8, ROWS), BF16)], axis=1)
    out_ref[ROWS:, :] = jnp.concatenate([upper, lower], axis=0)


def attend_first_kernel(step, place_ref, q_ref, mine_ref, other_ref, out_ref, k_ref, v_ref):
    place_keys(place_ref[0], mine_ref, other_ref, k_ref, v_ref)
    attend_kernel(step, place_ref, q_ref, k_ref, v_ref, out_ref)


def combine_kernel(own_ref, back1_ref, back2_ref, back3_ref, out_ref):
    refs = [own_ref, back1_ref, back2_ref, back3_ref]
    logs = []
    for ref in refs:
        tail = ref[ROWS:, :].astype(F32)
        logs.append(tail[:8, :ROWS] + tail[:8, ROWS:] + tail[8:, :ROWS])
    best = jnp.maximum(jnp.maximum(logs[0], logs[1]), jnp.maximum(logs[2], logs[3]))
    shares = [jnp.exp2(log - best) for log in logs]
    inverse = 1.0 / (shares[0] + shares[1] + shares[2] + shares[3])
    table = jnp.concatenate(
        [share * inverse for share in shares] + [jnp.zeros((128 - 32, ROWS), F32)], axis=0
    ).T
    for h in range(HEADS_Q):
        cols = slice(h * HD, (h + 1) * HD)
        total = jnp.zeros((ROWS, HD), F32)
        for i, ref in enumerate(refs):
            total += table[:, 8 * i + h : 8 * i + h + 1] * ref[:ROWS, cols].astype(F32)
        out_ref[:, cols] = total.astype(BF16)


def call(kernel, name, out_shape, in_specs, limit, flops, moved, streamed=False, **options):
    out_specs = jax.tree.map(lambda _: VM, out_shape)
    if streamed:
        options["grid"] = (1,)
        in_specs = [
            spec if spec in (SM, ANY) else pl.BlockSpec(spec, lambda i, n=len(spec): (0,) * n)
            for spec in in_specs
        ]
        out_specs = jax.tree.map(
            lambda out: pl.BlockSpec(out.shape, lambda i, n=len(out.shape): (0,) * n), out_shape
        )
    return pl.pallas_call(
        kernel,
        out_shape=out_shape,
        in_specs=in_specs,
        out_specs=out_specs,
        name=name,
        cost_estimate=pl.CostEstimate(flops=flops, bytes_accessed=moved, transcendentals=0),
        compiler_params=pltpu.CompilerParams(vmem_limit_bytes=limit * MIB),
        **options,
    )


def shape(dims, kind):
    return jax.ShapeDtypeStruct(dims, kind)


def swap(value, axis, size, step):
    return lax.ppermute(value, axis, [(i, i ^ step) for i in range(size)])


def exchange(chunks, axes):
    return lax.all_to_all(chunks, axes, 0, 0, tiled=True)


def after(kernel, inputs):
    def ordered(*refs):
        kernel(*refs[:inputs], *refs[inputs + 1 :])

    return ordered


def body(
    hidden_states,
    ssm_input,
    step_size,
    decay_rate,
    proj_b,
    proj_c,
    skip_gain,
    norm_gain,
    latent_from_ssm,
    latent_from_hidden,
    key_rebuild,
    value_rebuild,
    queries,
):
    place = jnp.stack(
        [lax.axis_index(axis) for axis in ("y", "x", "z", "core")]
    ).astype(jnp.int32)

    payload = call(
        state_kernel,
        "state",
        shape((NX, STATE, PAY), BF16),
        [SM, (ROWS, INNER), (HEADS_SSM, ROWS), (STATE, ROWS)],
        60,
        1 << 27,
        MIB,
        streamed=True,
    )(decay_rate, ssm_input, step_size, proj_b)
    spans = exchange(payload, "x")
    from_hidden = call(
        after(hidden_kernel, 2),
        "hidden",
        shape((ROWS, RANK), F32),
        [VM, VM, ANY],
        16,
        1 << 31,
        MIB,
    )(hidden_states, latent_from_hidden, payload)
    totals, before, row_decay = call(
        after(row_kernel, 2),
        "row",
        (
            shape((NY, STATE, PAY), BF16),
            shape((STATE, INNER), F32),
            shape((STATE, INNER), F32),
        ),
        [SM, VM, ANY],
        8,
        1 << 24,
        MIB // 2,
    )(place, spans, from_hidden)

    rows = exchange(totals, "y")
    partial, growth = call(
        after(intra_kernel, 6),
        "intra",
        (shape((ROWS, INNER), F32), shape((ROWS, 128), BF16)),
        [SM, SM] + [VM] * 4 + [ANY],
        24,
        1 << 31,
        3 * MIB,
    )(decay_rate, skip_gain, ssm_input, step_size, proj_b, proj_c, before)
    mamba_out, latent_terms = call(
        finish_kernel,
        "finish",
        (shape((ROWS, INNER), BF16), shape((ROWS, RANK), BF16)),
        [SM] + [VM] * 9,
        24,
        1 << 29,
        4 * MIB,
    )(
        place, rows, before, row_decay, partial, growth, proj_c, norm_gain.reshape(1, INNER),
        latent_from_ssm, from_hidden,
    )

    def copied(done):
        return call(
            after(copy_kernel, 1), "copy", shape(queries.shape, BF16), [VM, ANY], 8, 1 << 27, MIB
        )(queries, done)

    pieces = exchange(latent_terms.reshape(NT, PIECE, RANK), ("z", "core"))
    lent = copied(latent_terms)
    latents = call(
        after(sum_kernel, 1),
        "sum",
        shape((NY * NZ, PIECE, RANK), BF16),
        [VM, ANY],
        8,
        1 << 20,
        MIB // 2,
    )(pieces, lent)

    blocks = exchange(latents, ("y", "z")).reshape(NY, HALF, RANK)
    lent = copied(latents)
    visiting1 = swap(lent, "x", NX, 1)
    visiting3 = swap(lent, "x", NX, 3)
    visiting2 = swap(visiting1, "x", NX, 3)
    weights = pl.pallas_call(
        weights_kernel,
        out_shape=shape((RANK, 2 * HD), BF16),
        grid_spec=pltpu.PrefetchScalarGridSpec(
            num_scalar_prefetch=1,
            grid=(1,),
            in_specs=[pl.BlockSpec((RANK, HD), lambda i, place: (0, place[2]))] * 2 + [ANY],
            out_specs=pl.BlockSpec((RANK, 2 * HD), lambda i, place: (0, 0)),
        ),
        name="weights",
        cost_estimate=pl.CostEstimate(flops=1 << 30, bytes_accessed=MIB, transcendentals=0),
        compiler_params=pltpu.CompilerParams(vmem_limit_bytes=8 * MIB),
    )(place, key_rebuild, value_rebuild, latents)
    mine = call(
        after(after(after(rebuild_kernel, 3), 3), 3),
        "rebuild",
        shape((NY * HALF, 2 * HD), BF16),
        [SM, VM, VM, ANY, ANY, ANY],
        8,
        1 << 27,
        MIB,
    )(place, blocks, weights, visiting1, visiting2, visiting3)
    other = swap(mine, "core", NC, 1)

    work = 4 * ROWS * HEADS_Q * HD * NY * ROWS
    answer = shape((ROWS + 16, HEADS_Q * HD), BF16)
    wide = shape((NY * ROWS, 2 * HD), BF16)
    done, keys, values = call(
        functools.partial(attend_first_kernel, 2), "attend", (answer, wide, wide),
        [SM, VM, VM, VM], 24, work, 4 * MIB,
    )(place, visiting2, mine, other)
    back = {2: swap(done, "x", NX, 2)}
    for step, query, awaited in ((1, visiting1, None), (3, visiting3, None), (0, queries, 2)):
        kernel = functools.partial(attend_kernel, step)
        operands = [place, query, keys, values, done]
        if awaited is not None:
            operands.append(back[awaited])
            kernel = after(kernel, 4)
        done = call(
            after(kernel, 4), "attend", answer, [SM, VM, VM, VM] + [ANY] * (len(operands) - 4),
            24, work, 4 * MIB,
        )(*operands)
        if step:
            back[step] = swap(done, "x", NX, step)

    attended = call(
        combine_kernel,
        "combine",
        shape((ROWS, HEADS_Q * HD), BF16),
        [VM] * 4,
        16,
        1 << 20,
        2 * MIB,
    )(done, back[1], back[2], back[3])
    return (mamba_out, attended)


def solution(mesh):
    grid = Mesh(mesh.devices.reshape(NY, NX, NZ, NC), ("y", "x", "z", "core"))
    ctx, tp = ("y", "x"), ("z", "core")
    return jax.shard_map(
        body,
        mesh=grid,
        in_specs=(
            P(ctx, tp),
            P(ctx, tp),
            P(tp, ctx),
            P(tp),
            P(None, ctx),
            P(None, ctx),
            P(tp),
            P(tp),
            P(tp, None),
            P(tp, None),
            P(),
            P(),
            P(ctx, tp),
        ),
        out_specs=(P(ctx, tp), P(ctx, tp)),
        check_vma=False,
    )
```

```python
import functools
import math

import jax
import jax.numpy as jnp
from jax import lax
from jax.experimental import pallas as pl
from jax.experimental.pallas import tpu as pltpu
from jax.sharding import Mesh
from jax.sharding import PartitionSpec as P

STATE = 16
HEADDIM = 64
ROWS = 256
HEADS_SSM = 16
INNER = HEADS_SSM * HEADDIM
HD = 128
RANK = 256
HEADS_Q = 4
NY, NX, NZ, NC = 8, 4, 8, 2
NT = NZ * NC
PIECE = ROWS // NT
HALF = ROWS // NC
NCTX = NY * NX
PAY = INNER + 128
BLOCKS = INNER // 128

NEG_BIG = -1e30
EPSILON = 1e-05
SCALE2 = math.log2(math.e) / math.sqrt(HD)
F32 = jnp.float32
BF16 = jnp.bfloat16
MIB = 1 << 20

VM = pl.BlockSpec(memory_space=pltpu.VMEM)
ANY = pl.BlockSpec(memory_space=pl.ANY)
SM = pl.BlockSpec(memory_space=pltpu.SMEM)


def iota(shape, axis):
    return lax.broadcasted_iota(jnp.int32, shape, axis)


def dot(a, b):
    return jnp.dot(a, b, preferred_element_type=F32)


def split(value):
    high = value.astype(BF16)
    return high, (value - high.astype(F32)).astype(BF16)


def spread():
    lane = iota((128, INNER), 0)
    head = iota((128, INNER), 1) // HEADDIM
    return jnp.where((lane < 2 * HEADS_SSM) & ((lane & 15) == head), 1.0, 0.0).astype(BF16)


def within_rows(step_ref, rate_ref):
    row = iota((HEADS_SSM, ROWS), 0)
    lane = iota((HEADS_SSM, ROWS), 1)
    rate = jnp.zeros((HEADS_SSM, ROWS), F32)
    for h in range(HEADS_SSM):
        rate = jnp.where(row == h, rate_ref[h], rate)
    total = -rate * step_ref[...]
    shift = 1
    while shift < ROWS:
        total = total + jnp.where(lane >= shift, pltpu.roll(total, shift, 1), 0.0)
        shift *= 2
    return total


def pack_decay(compact):
    lane = iota(compact.shape, 1)
    kept = jnp.where(lane < HEADS_SSM, compact, 0.0)
    high = kept.astype(BF16).astype(F32)
    low = pltpu.roll(kept - high, HEADS_SSM, 1)
    return (high + low).astype(BF16)


def unpack_decay(packed):
    value = packed.astype(F32)
    lane = iota(value.shape, 1)
    return jnp.where(lane < HEADS_SSM, value + pltpu.roll(value, 128 - HEADS_SSM, 1), 0.0)


def state_kernel(rate_ref, x_ref, step_ref, b_ref, pay_ref):
    within = within_rows(step_ref, rate_ref)
    last = within[:, ROWS - 1 : ROWS]
    to_end = jnp.exp(last - within)
    b = b_ref[...].astype(F32)
    lane = iota((STATE, 128), 1)
    for j in range(BLOCKS):
        cols = slice(128 * j, 128 * (j + 1))
        a0h, a0l = split(to_end[2 * j : 2 * j + 1, :] * b)
        a1h, a1l = split(to_end[2 * j + 1 : 2 * j + 2, :] * b)
        lhs = jnp.concatenate([a0h, a1h, a0l, a1l], axis=0)
        out = dot(lhs, x_ref[:, cols])
        both = out[: 2 * STATE] + out[2 * STATE :]
        state = jnp.where(lane < HEADDIM, both[:STATE], both[STATE:])
        for i in range(NX):
            pay_ref[i, :, cols] = state.astype(BF16)
    head = iota((HEADS_SSM, 128), 0)
    hlane = iota((HEADS_SSM, 128), 1)
    compact = jnp.sum(jnp.where(hlane == head, jnp.exp(last), 0.0), axis=0, keepdims=True)
    packed = pack_decay(jnp.broadcast_to(compact, (STATE, 128)))
    for i in range(NX):
        pay_ref[i, :, INNER:] = packed


def widened(spans_ref, count):
    packed = jnp.concatenate([spans_ref[i, :, INNER:] for i in range(count)], axis=0)
    wide = dot(packed, spread())
    return [wide[i * STATE : (i + 1) * STATE] for i in range(count)]


def row_kernel(place_ref, spans_ref, total_ref, before_ref, decay_ref):
    x = place_ref[1]
    wide = widened(spans_ref, NX)
    run = jnp.zeros((STATE, INNER), F32)
    before = run
    before_decay = jnp.ones((STATE, INNER), F32)
    compact = jnp.ones((STATE, 128), F32)
    for i in range(NX):
        run = wide[i] * run + spans_ref[i, :, :INNER].astype(F32)
        before = jnp.where(i < x, run, before)
        before_decay = jnp.where(i < x, wide[i] * before_decay, before_decay)
        compact = compact * unpack_decay(spans_ref[i, :, INNER:])
    before_ref[...] = before
    decay_ref[...] = before_decay
    total = run.astype(BF16)
    packed = pack_decay(compact)
    for i in range(NY):
        total_ref[i, :, :INNER] = total
        total_ref[i, :, INNER:] = packed


def intra_kernel(
    rate_ref, skip_ref, x_ref, step_ref, b_ref, c_ref, y_ref, grow_ref
):
    within = within_rows(step_ref, rate_ref)
    columns = jnp.concatenate([within, jnp.zeros((128 - HEADS_SSM, ROWS), F32)], axis=0).T
    grow = jnp.exp(columns)
    grow_ref[...] = pack_decay(grow)
    meet = lax.dot_general(
        c_ref[...], b_ref[...], (((0,), (0,)), ((), ())), preferred_element_type=F32
    )
    half = ROWS // 2
    causal = iota((half, half), 0) >= iota((half, half), 1)
    lane = iota((ROWS, 128), 1)
    zeros = jnp.zeros((half, half), BF16)

    def mixing(h):
        row = within[h : h + 1, :]
        column = columns[:, h : h + 1]
        top, bottom = column[:half], column[half:]
        left, right = row[:, :half], row[:, half:]
        m00 = meet[:half, :half] * jnp.exp(jnp.where(causal, top - left, NEG_BIG))
        m10 = meet[half:, :half] * jnp.exp(bottom - left)
        m11 = meet[half:, half:] * jnp.exp(jnp.where(causal, bottom - right, NEG_BIG))
        upper = jnp.concatenate([m00.astype(BF16), zeros], axis=1)
        lower = jnp.concatenate([m10.astype(BF16), m11.astype(BF16)], axis=1)
        return jnp.concatenate([upper, lower], axis=0)

    for j in range(HEADS_SSM // 2):
        cols = slice(128 * j, 128 * (j + 1))
        x = x_ref[:, cols]
        out0 = dot(mixing(2 * j), x)
        out1 = dot(mixing(2 * j + 1), x)
        skip = jnp.where(lane < HEADDIM, skip_ref[2 * j], skip_ref[2 * j + 1])
        y_ref[:, cols] = jnp.where(lane < HEADDIM, out0, out1) + skip * x.astype(F32)


def finish_kernel(
    place_ref, rows_ref, before_ref, decay_ref, y_ref, grow_ref, c_ref, gain_ref, w_ref, h_ref,
    mamba_ref, part_ref,
):
    chan = spread()
    wide = widened(rows_ref, NY - 1)
    run = jnp.zeros((STATE, INNER), F32)
    for row in range(NY - 1):
        joined = wide[row] * run + rows_ref[row, :, :INNER].astype(F32)
        run = jnp.where(row < place_ref[0], joined, run)
    carried = run * decay_ref[...] + before_ref[...]
    high, low = split(carried)
    c = c_ref[...]
    from_state = lax.dot_general(
        jnp.concatenate([c, c], axis=0),
        jnp.concatenate([high, low], axis=0),
        (((0,), (0,)), ((), ())),
        preferred_element_type=F32,
    )
    grow = dot(grow_ref[...], chan)
    out = y_ref[...] + from_state * grow
    gather = jnp.where(
        iota((INNER, 128), 0) // HEADDIM == iota((INNER, 128), 1), 1.0, 0.0
    ).astype(BF16)
    square = dot((out * out).astype(BF16), gather) * (1.0 / HEADDIM)
    inverse = dot(pack_decay(lax.rsqrt(square + EPSILON)), chan)
    mamba = (out * inverse * gain_ref[...]).astype(BF16)
    mamba_ref[...] = mamba
    part_ref[...] = (dot(mamba, w_ref[...]) + h_ref[...]).astype(BF16)


def copy_kernel(q_ref, out_ref):
    out_ref[...] = q_ref[...]


def sum_kernel(pieces_ref, out_ref):
    total = pieces_ref[0].astype(F32)
    for i in range(1, NT):
        total = total + pieces_ref[i].astype(F32)
    rounded = total.astype(BF16)
    for i in range(NY * NZ):
        out_ref[i] = rounded


def hidden_kernel(hidden_ref, w_ref, out_ref):
    out_ref[...] = dot(hidden_ref[...], w_ref[...])


def weights_kernel(place_ref, wk_ref, wv_ref, order_ref, out_ref):
    out_ref[:, :HD] = wk_ref[...]
    out_ref[:, HD:] = wv_ref[...]


def rebuild_kernel(place_ref, mine_ref, w_ref, out_ref):
    y = place_ref[0]
    w = w_ref[...]
    for block in range(NY):
        begin = ((y - block) & (NY - 1)) * HALF
        out = pl.ds(pl.multiple_of(begin, HALF), HALF)
        rows = dot(mine_ref[block], w)
        out_ref[out, :HD] = (rows[:, :HD] * SCALE2).astype(BF16)
        out_ref[out, HD:] = rows[:, HD:].astype(BF16)


def place_keys(y, mine_ref, other_ref, k_ref, v_ref):
    lane = iota((HALF, HD), 1)
    ones = jnp.ones((HALF, HD), BF16)
    for part, ref in enumerate((mine_ref, other_ref)):
        for block in range(NY):
            rows = slice(block * HALF, (block + 1) * HALF)
            out = slice((part * NY + block) * HALF, (part * NY + block + 1) * HALF)
            bias = jnp.where(y >= block, 0.0, NEG_BIG)
            k_ref[out, :HD] = ref[rows, :HD]
            k_ref[out, HD:] = jnp.where(lane == 0, bias, 0.0).astype(BF16)
            v_ref[out, :HD] = ref[rows, HD:]
            v_ref[out, HD:] = ones


def attend_kernel(step, place_ref, q_ref, k_ref, v_ref, out_ref):
    x, core = place_ref[1], place_ref[3]
    ahead = ((x ^ step) - x) * ROWS
    lane = iota((ROWS, 128), 1)
    unit = jnp.where(lane == 0, 1.0, 0.0).astype(BF16)
    token = iota((ROWS, HALF), 0) + ahead
    slot = iota((ROWS, HALF), 1)
    allowed = []
    for own in (core, 1 - core):
        key = (slot // PIECE) * (2 * PIECE) + own * PIECE + (slot & (PIECE - 1))
        allowed.append(key <= token)

    def scored(first):
        query = jnp.concatenate(
            [
                jnp.concatenate([q_ref[:, h * HD : (h + 1) * HD], unit], axis=1)
                for h in (first, first + 1)
            ],
            axis=0,
        )
        return lax.dot_general(
            query, k_ref[...], (((1,), (1,)), ((), ())), preferred_element_type=F32
        )

    allowed = [jnp.concatenate([part, part], axis=0) for part in allowed]
    stats = jnp.zeros((ROWS, 128), F32)
    following = scored(0)
    for first in range(0, HEADS_Q, 2):
        scores = following
        if first + 2 < HEADS_Q:
            following = scored(first + 2)
        pieces = []
        for part in range(2):
            begin = part * NY * HALF
            pieces.append(jnp.where(allowed[part], scores[:, begin : begin + HALF], NEG_BIG))
            pieces.append(scores[:, begin + HALF : begin + NY * HALF])
        scores = jnp.concatenate(pieces, axis=1)
        best = jnp.max(scores, axis=1, keepdims=True)
        weights = jnp.exp2((scores - best).astype(BF16))
        sums = dot(weights, v_ref[...])
        norm = sums[:, HD:]
        ratio = (sums[:, :HD] / norm).astype(BF16)
        level = best + jnp.log2(norm)
        for h in (first, first + 1):
            rows = slice((h - first) * ROWS, (h - first + 1) * ROWS)
            out_ref[:ROWS, h * HD : (h + 1) * HD] = ratio[rows]
            stats = jnp.where(lane == h, level[rows], stats)
    rows = stats.T[:8, :]
    high, mid = split(rows)
    low = (rows - high.astype(F32) - mid.astype(F32)).astype(BF16)
    upper = jnp.concatenate([high, mid], axis=1)
    lower = jnp.concatenate([low, jnp.zeros((8, ROWS), BF16)], axis=1)
    out_ref[ROWS:, :] = jnp.concatenate([upper, lower], axis=0)


def attend_first_kernel(step, place_ref, q_ref, mine_ref, other_ref, out_ref, k_ref, v_ref):
    place_keys(place_ref[0], mine_ref, other_ref, k_ref, v_ref)
    attend_kernel(step, place_ref, q_ref, k_ref, v_ref, out_ref)


def combine_kernel(own_ref, back1_ref, back2_ref, back3_ref, out_ref):
    refs = [own_ref, back1_ref, back2_ref, back3_ref]
    logs = []
    for ref in refs:
        tail = ref[ROWS:, :].astype(F32)
        logs.append(tail[:8, :ROWS] + tail[:8, ROWS:] + tail[8:, :ROWS])
    best = jnp.maximum(jnp.maximum(logs[0], logs[1]), jnp.maximum(logs[2], logs[3]))
    shares = [jnp.exp2(log - best) for log in logs]
    inverse = 1.0 / (shares[0] + shares[1] + shares[2] + shares[3])
    table = jnp.concatenate(
        [share * inverse for share in shares] + [jnp.zeros((128 - 32, ROWS), F32)], axis=0
    ).T
    for h in range(HEADS_Q):
        cols = slice(h * HD, (h + 1) * HD)
        total = jnp.zeros((ROWS, HD), F32)
        for i, ref in enumerate(refs):
            total += table[:, 8 * i + h : 8 * i + h + 1] * ref[:ROWS, cols].astype(F32)
        out_ref[:, cols] = total.astype(BF16)


def call(kernel, name, out_shape, in_specs, limit, flops, moved, streamed=False, **options):
    out_specs = jax.tree.map(lambda _: VM, out_shape)
    if streamed:
        options["grid"] = (1,)
        in_specs = [
            spec if spec in (SM, ANY) else pl.BlockSpec(spec, lambda i, n=len(spec): (0,) * n)
            for spec in in_specs
        ]
        out_specs = jax.tree.map(
            lambda out: pl.BlockSpec(out.shape, lambda i, n=len(out.shape): (0,) * n), out_shape
        )
    return pl.pallas_call(
        kernel,
        out_shape=out_shape,
        in_specs=in_specs,
        out_specs=out_specs,
        name=name,
        cost_estimate=pl.CostEstimate(flops=flops, bytes_accessed=moved, transcendentals=0),
        compiler_params=pltpu.CompilerParams(vmem_limit_bytes=limit * MIB),
        **options,
    )


def shape(dims, kind):
    return jax.ShapeDtypeStruct(dims, kind)


def swap(value, axis, size, step):
    return lax.ppermute(value, axis, [(i, i ^ step) for i in range(size)])


def exchange(chunks, axes):
    return lax.all_to_all(chunks, axes, 0, 0, tiled=True)


def after(kernel, inputs):
    def ordered(*refs):
        kernel(*refs[:inputs], *refs[inputs + 1 :])

    return ordered


def body(
    hidden_states,
    ssm_input,
    step_size,
    decay_rate,
    proj_b,
    proj_c,
    skip_gain,
    norm_gain,
    latent_from_ssm,
    latent_from_hidden,
    key_rebuild,
    value_rebuild,
    queries,
):
    place = jnp.stack(
        [lax.axis_index(axis) for axis in ("y", "x", "z", "core")]
    ).astype(jnp.int32)

    payload = call(
        state_kernel,
        "state",
        shape((NX, STATE, PAY), BF16),
        [SM, (ROWS, INNER), (HEADS_SSM, ROWS), (STATE, ROWS)],
        60,
        1 << 27,
        MIB,
        streamed=True,
    )(decay_rate, ssm_input, step_size, proj_b)
    spans = exchange(payload, "x")
    from_hidden = call(
        after(hidden_kernel, 2),
        "hidden",
        shape((ROWS, RANK), F32),
        [VM, VM, ANY],
        16,
        1 << 31,
        MIB,
    )(hidden_states, latent_from_hidden, payload)
    totals, before, row_decay = call(
        after(row_kernel, 2),
        "row",
        (
            shape((NY, STATE, PAY), BF16),
            shape((STATE, INNER), F32),
            shape((STATE, INNER), F32),
        ),
        [SM, VM, ANY],
        8,
        1 << 24,
        MIB // 2,
    )(place, spans, from_hidden)

    rows = exchange(totals, "y")
    partial, growth = call(
        after(intra_kernel, 6),
        "intra",
        (shape((ROWS, INNER), F32), shape((ROWS, 128), BF16)),
        [SM, SM] + [VM] * 4 + [ANY],
        24,
        1 << 31,
        3 * MIB,
    )(decay_rate, skip_gain, ssm_input, step_size, proj_b, proj_c, before)
    mamba_out, latent_terms = call(
        finish_kernel,
        "finish",
        (shape((ROWS, INNER), BF16), shape((ROWS, RANK), BF16)),
        [SM] + [VM] * 9,
        24,
        1 << 29,
        4 * MIB,
    )(
        place, rows, before, row_decay, partial, growth, proj_c, norm_gain.reshape(1, INNER),
        latent_from_ssm, from_hidden,
    )

    def copied(done):
        return call(
            after(copy_kernel, 1), "copy", shape(queries.shape, BF16), [VM, ANY], 8, 1 << 27, MIB
        )(queries, done)

    pieces = exchange(latent_terms.reshape(NT, PIECE, RANK), ("z", "core"))
    lent = copied(latent_terms)
    latents = call(
        after(sum_kernel, 1),
        "sum",
        shape((NY * NZ, PIECE, RANK), BF16),
        [VM, ANY],
        8,
        1 << 20,
        MIB // 2,
    )(pieces, lent)

    blocks = exchange(latents, ("y", "z")).reshape(NY, HALF, RANK)
    lent = copied(latents)
    visiting1 = swap(lent, "x", NX, 1)
    visiting3 = swap(lent, "x", NX, 3)
    visiting2 = swap(visiting1, "x", NX, 3)
    weights = pl.pallas_call(
        weights_kernel,
        out_shape=shape((RANK, 2 * HD), BF16),
        grid_spec=pltpu.PrefetchScalarGridSpec(
            num_scalar_prefetch=1,
            grid=(1,),
            in_specs=[pl.BlockSpec((RANK, HD), lambda i, place: (0, place[2]))] * 2 + [ANY],
            out_specs=pl.BlockSpec((RANK, 2 * HD), lambda i, place: (0, 0)),
        ),
        name="weights",
        cost_estimate=pl.CostEstimate(flops=1 << 30, bytes_accessed=MIB, transcendentals=0),
        compiler_params=pltpu.CompilerParams(vmem_limit_bytes=8 * MIB),
    )(place, key_rebuild, value_rebuild, latents)
    mine = call(
        after(after(rebuild_kernel, 3), 3),
        "rebuild",
        shape((NY * HALF, 2 * HD), BF16),
        [SM, VM, VM, ANY, ANY],
        8,
        1 << 27,
        MIB,
    )(place, blocks, weights, visiting1, visiting3)
    other = swap(mine, "core", NC, 1)

    work = 4 * ROWS * HEADS_Q * HD * NY * ROWS
    answer = shape((ROWS + 16, HEADS_Q * HD), BF16)
    wide = shape((NY * ROWS, 2 * HD), BF16)
    done, keys, values = call(
        functools.partial(attend_first_kernel, 1), "attend", (answer, wide, wide),
        [SM, VM, VM, VM], 24, work, 4 * MIB,
    )(place, visiting1, mine, other)
    back = {1: swap(done, "x", NX, 1)}
    for step, query, awaited in ((2, visiting2, None), (3, visiting3, 1), (0, queries, None)):
        kernel = functools.partial(attend_kernel, step)
        operands = [place, query, keys, values, done]
        if awaited is not None:
            operands.append(back[awaited])
            kernel = after(kernel, 4)
        done = call(
            after(kernel, 4), "attend", answer, [SM, VM, VM, VM] + [ANY] * (len(operands) - 4),
            24, work, 4 * MIB,
        )(*operands)
        if step:
            back[step] = swap(done, "x", NX, step)

    attended = call(
        combine_kernel,
        "combine",
        shape((ROWS, HEADS_Q * HD), BF16),
        [VM] * 4,
        16,
        1 << 20,
        2 * MIB,
    )(done, back[1], back[2], back[3])
    return (mamba_out, attended)


def solution(mesh):
    grid = Mesh(mesh.devices.reshape(NY, NX, NZ, NC), ("y", "x", "z", "core"))
    ctx, tp = ("y", "x"), ("z", "core")
    return jax.shard_map(
        body,
        mesh=grid,
        in_specs=(
            P(ctx, tp),
            P(ctx, tp),
            P(tp, ctx),
            P(tp),
            P(None, ctx),
            P(None, ctx),
            P(tp),
            P(tp),
            P(tp, None),
            P(tp, None),
            P(),
            P(),
            P(ctx, tp),
        ),
        out_specs=(P(ctx, tp), P(ctx, tp)),
        check_vma=False,
    )
```

```python
import functools
import math

import jax
import jax.numpy as jnp
from jax import lax
from jax.experimental import pallas as pl
from jax.experimental.pallas import tpu as pltpu
from jax.sharding import Mesh
from jax.sharding import PartitionSpec as P

STATE = 16
HEADDIM = 64
ROWS = 256
HEADS_SSM = 16
INNER = HEADS_SSM * HEADDIM
HD = 128
RANK = 256
HEADS_Q = 4
NY, NX, NZ, NC = 8, 4, 8, 2
NT = NZ * NC
PIECE = ROWS // NT
HALF = ROWS // NC
NCTX = NY * NX
PAY = INNER + 128
BLOCKS = INNER // 128

NEG_BIG = -1e30
EPSILON = 1e-05
SCALE2 = math.log2(math.e) / math.sqrt(HD)
F32 = jnp.float32
BF16 = jnp.bfloat16
MIB = 1 << 20

VM = pl.BlockSpec(memory_space=pltpu.VMEM)
ANY = pl.BlockSpec(memory_space=pl.ANY)
SM = pl.BlockSpec(memory_space=pltpu.SMEM)


def iota(shape, axis):
    return lax.broadcasted_iota(jnp.int32, shape, axis)


def dot(a, b):
    return jnp.dot(a, b, preferred_element_type=F32)


def split(value):
    high = value.astype(BF16)
    return high, (value - high.astype(F32)).astype(BF16)


def spread():
    lane = iota((128, INNER), 0)
    head = iota((128, INNER), 1) // HEADDIM
    return jnp.where((lane < 2 * HEADS_SSM) & ((lane & 15) == head), 1.0, 0.0).astype(BF16)


def within_rows(step_ref, rate_ref):
    row = iota((HEADS_SSM, ROWS), 0)
    lane = iota((HEADS_SSM, ROWS), 1)
    rate = jnp.zeros((HEADS_SSM, ROWS), F32)
    for h in range(HEADS_SSM):
        rate = jnp.where(row == h, rate_ref[h], rate)
    total = -rate * step_ref[...]
    shift = 1
    while shift < ROWS:
        total = total + jnp.where(lane >= shift, pltpu.roll(total, shift, 1), 0.0)
        shift *= 2
    return total


def pack_decay(compact):
    lane = iota(compact.shape, 1)
    kept = jnp.where(lane < HEADS_SSM, compact, 0.0)
    high = kept.astype(BF16).astype(F32)
    low = pltpu.roll(kept - high, HEADS_SSM, 1)
    return (high + low).astype(BF16)


def unpack_decay(packed):
    value = packed.astype(F32)
    lane = iota(value.shape, 1)
    return jnp.where(lane < HEADS_SSM, value + pltpu.roll(value, 128 - HEADS_SSM, 1), 0.0)


def state_kernel(rate_ref, x_ref, step_ref, b_ref, pay_ref):
    within = within_rows(step_ref, rate_ref)
    last = within[:, ROWS - 1 : ROWS]
    to_end = jnp.exp(last - within)
    b = b_ref[...].astype(F32)
    lane = iota((STATE, 128), 1)
    for j in range(BLOCKS):
        cols = slice(128 * j, 128 * (j + 1))
        a0h, a0l = split(to_end[2 * j : 2 * j + 1, :] * b)
        a1h, a1l = split(to_end[2 * j + 1 : 2 * j + 2, :] * b)
        lhs = jnp.concatenate([a0h, a1h, a0l, a1l], axis=0)
        out = dot(lhs, x_ref[:, cols])
        both = out[: 2 * STATE] + out[2 * STATE :]
        state = jnp.where(lane < HEADDIM, both[:STATE], both[STATE:])
        for i in range(NX):
            pay_ref[i, :, cols] = state.astype(BF16)
    head = iota((HEADS_SSM, 128), 0)
    hlane = iota((HEADS_SSM, 128), 1)
    compact = jnp.sum(jnp.where(hlane == head, jnp.exp(last), 0.0), axis=0, keepdims=True)
    packed = pack_decay(jnp.broadcast_to(compact, (STATE, 128)))
    for i in range(NX):
        pay_ref[i, :, INNER:] = packed


def widened(spans_ref, count):
    packed = jnp.concatenate([spans_ref[i, :, INNER:] for i in range(count)], axis=0)
    wide = dot(packed, spread())
    return [wide[i * STATE : (i + 1) * STATE] for i in range(count)]


def row_kernel(place_ref, spans_ref, total_ref, before_ref, decay_ref):
    x = place_ref[1]
    wide = widened(spans_ref, NX)
    run = jnp.zeros((STATE, INNER), F32)
    before = run
    before_decay = jnp.ones((STATE, INNER), F32)
    compact = jnp.ones((STATE, 128), F32)
    for i in range(NX):
        run = wide[i] * run + spans_ref[i, :, :INNER].astype(F32)
        before = jnp.where(i < x, run, before)
        before_decay = jnp.where(i < x, wide[i] * before_decay, before_decay)
        compact = compact * unpack_decay(spans_ref[i, :, INNER:])
    before_ref[...] = before
    decay_ref[...] = before_decay
    total = run.astype(BF16)
    packed = pack_decay(compact)
    for i in range(NY):
        total_ref[i, :, :INNER] = total
        total_ref[i, :, INNER:] = packed


def intra_kernel(
    rate_ref, skip_ref, x_ref, step_ref, b_ref, c_ref, y_ref, grow_ref
):
    within = within_rows(step_ref, rate_ref)
    columns = jnp.concatenate([within, jnp.zeros((128 - HEADS_SSM, ROWS), F32)], axis=0).T
    grow = jnp.exp(columns)
    grow_ref[...] = pack_decay(grow)
    meet = lax.dot_general(
        c_ref[...], b_ref[...], (((0,), (0,)), ((), ())), preferred_element_type=F32
    )
    half = ROWS // 2
    causal = iota((half, half), 0) >= iota((half, half), 1)
    lane = iota((ROWS, 128), 1)
    zeros = jnp.zeros((half, half), BF16)

    def mixing(h):
        row = within[h : h + 1, :]
        column = columns[:, h : h + 1]
        top, bottom = column[:half], column[half:]
        left, right = row[:, :half], row[:, half:]
        m00 = meet[:half, :half] * jnp.exp(jnp.where(causal, top - left, NEG_BIG))
        m10 = meet[half:, :half] * jnp.exp(bottom - left)
        m11 = meet[half:, half:] * jnp.exp(jnp.where(causal, bottom - right, NEG_BIG))
        upper = jnp.concatenate([m00.astype(BF16), zeros], axis=1)
        lower = jnp.concatenate([m10.astype(BF16), m11.astype(BF16)], axis=1)
        return jnp.concatenate([upper, lower], axis=0)

    for j in range(HEADS_SSM // 2):
        cols = slice(128 * j, 128 * (j + 1))
        x = x_ref[:, cols]
        out0 = dot(mixing(2 * j), x)
        out1 = dot(mixing(2 * j + 1), x)
        skip = jnp.where(lane < HEADDIM, skip_ref[2 * j], skip_ref[2 * j + 1])
        y_ref[:, cols] = jnp.where(lane < HEADDIM, out0, out1) + skip * x.astype(F32)


def finish_kernel(
    place_ref, rows_ref, before_ref, decay_ref, y_ref, grow_ref, c_ref, gain_ref, w_ref, h_ref,
    mamba_ref, part_ref,
):
    chan = spread()
    wide = widened(rows_ref, NY - 1)
    run = jnp.zeros((STATE, INNER), F32)
    for row in range(NY - 1):
        joined = wide[row] * run + rows_ref[row, :, :INNER].astype(F32)
        run = jnp.where(row < place_ref[0], joined, run)
    carried = run * decay_ref[...] + before_ref[...]
    high, low = split(carried)
    c = c_ref[...]
    from_state = lax.dot_general(
        jnp.concatenate([c, c], axis=0),
        jnp.concatenate([high, low], axis=0),
        (((0,), (0,)), ((), ())),
        preferred_element_type=F32,
    )
    grow = dot(grow_ref[...], chan)
    out = y_ref[...] + from_state * grow
    gather = jnp.where(
        iota((INNER, 128), 0) // HEADDIM == iota((INNER, 128), 1), 1.0, 0.0
    ).astype(BF16)
    square = dot((out * out).astype(BF16), gather) * (1.0 / HEADDIM)
    inverse = dot(pack_decay(lax.rsqrt(square + EPSILON)), chan)
    mamba = (out * inverse * gain_ref[...]).astype(BF16)
    mamba_ref[...] = mamba
    part_ref[...] = (dot(mamba, w_ref[...]) + h_ref[...]).astype(BF16)


def copy_kernel(q_ref, out_ref):
    out_ref[...] = q_ref[...]


def sum_kernel(pieces_ref, out_ref):
    total = pieces_ref[0].astype(F32)
    for i in range(1, NT):
        total = total + pieces_ref[i].astype(F32)
    rounded = total.astype(BF16)
    for i in range(NY * NZ):
        out_ref[i] = rounded


def hidden_kernel(hidden_ref, w_ref, out_ref):
    out_ref[...] = dot(hidden_ref[...], w_ref[...])


def weights_kernel(place_ref, wk_ref, wv_ref, order_ref, out_ref):
    out_ref[:, :HD] = wk_ref[...]
    out_ref[:, HD:] = wv_ref[...]


def rebuild_kernel(place_ref, mine_ref, w_ref, out_ref):
    y = place_ref[0]
    w = w_ref[...]
    for block in range(NY):
        begin = ((y - block) & (NY - 1)) * HALF
        out = pl.ds(pl.multiple_of(begin, HALF), HALF)
        rows = dot(mine_ref[block], w)
        out_ref[out, :HD] = (rows[:, :HD] * SCALE2).astype(BF16)
        out_ref[out, HD:] = rows[:, HD:].astype(BF16)


def place_keys(y, mine_ref, other_ref, k_ref, v_ref):
    lane = iota((HALF, HD), 1)
    ones = jnp.ones((HALF, HD), BF16)
    for part, ref in enumerate((mine_ref, other_ref)):
        for block in range(NY):
            rows = slice(block * HALF, (block + 1) * HALF)
            out = slice((part * NY + block) * HALF, (part * NY + block + 1) * HALF)
            bias = jnp.where(y >= block, 0.0, NEG_BIG)
            k_ref[out, :HD] = ref[rows, :HD]
            near = 1.0 if block == 0 else 0.0
            k_ref[out, HD:] = jnp.where(
                lane == 0, bias, jnp.where(lane == 1, near, 0.0)
            ).astype(BF16)
            v_ref[out, :HD] = ref[rows, HD:]
            v_ref[out, HD:] = ones


def own_masked(scores, core):
    token = iota((2 * ROWS, HALF), 0) & (ROWS - 1)
    slot = iota((2 * ROWS, HALF), 1)
    pieces = []
    for part, own in enumerate((core, 1 - core)):
        key = (slot // PIECE) * (2 * PIECE) + own * PIECE + (slot & (PIECE - 1))
        begin = part * NY * HALF
        pieces.append(jnp.where(key <= token, scores[:, begin : begin + HALF], NEG_BIG))
        pieces.append(scores[:, begin + HALF : begin + NY * HALF])
    return jnp.concatenate(pieces, axis=1)


def attend_kernel(step, place_ref, q_ref, k_ref, v_ref, out_ref):
    x, core = place_ref[1], place_ref[3]
    lane = iota((ROWS, 128), 1)
    behind = jnp.where((x ^ step) < x, NEG_BIG, 0.0)
    unit = jnp.where(lane == 0, 1.0, jnp.where(lane == 1, behind, 0.0)).astype(BF16)

    def scored(first):
        query = jnp.concatenate(
            [
                jnp.concatenate([q_ref[:, h * HD : (h + 1) * HD], unit], axis=1)
                for h in (first, first + 1)
            ],
            axis=0,
        )
        return lax.dot_general(
            query, k_ref[...], (((1,), (1,)), ((), ())), preferred_element_type=F32
        )

    stats = jnp.zeros((ROWS, 128), F32)
    following = scored(0)
    for first in range(0, HEADS_Q, 2):
        scores = following
        if first + 2 < HEADS_Q:
            following = scored(first + 2)
        if step == 0:
            scores = own_masked(scores, core)
        best = jnp.max(scores, axis=1, keepdims=True)
        weights = jnp.exp2(scores - best).astype(BF16)
        sums = dot(weights, v_ref[...])
        norm = sums[:, HD:]
        ratio = (sums[:, :HD] / norm).astype(BF16)
        level = best + jnp.log2(norm)
        for h in (first, first + 1):
            rows = slice((h - first) * ROWS, (h - first + 1) * ROWS)
            out_ref[:ROWS, h * HD : (h + 1) * HD] = ratio[rows]
            stats = jnp.where(lane == h, level[rows], stats)
    rows = stats.T[:8, :]
    high, mid = split(rows)
    low = (rows - high.astype(F32) - mid.astype(F32)).astype(BF16)
    upper = jnp.concatenate([high, mid], axis=1)
    lower = jnp.concatenate([low, jnp.zeros((8, ROWS), BF16)], axis=1)
    out_ref[ROWS:, :] = jnp.concatenate([upper, lower], axis=0)


def attend_first_kernel(step, place_ref, q_ref, mine_ref, other_ref, out_ref, k_ref, v_ref):
    place_keys(place_ref[0], mine_ref, other_ref, k_ref, v_ref)
    attend_kernel(step, place_ref, q_ref, k_ref, v_ref, out_ref)


def combine_kernel(own_ref, back1_ref, back2_ref, back3_ref, out_ref):
    refs = [own_ref, back1_ref, back2_ref, back3_ref]
    logs = []
    for ref in refs:
        tail = ref[ROWS:, :].astype(F32)
        logs.append(tail[:8, :ROWS] + tail[:8, ROWS:] + tail[8:, :ROWS])
    best = jnp.maximum(jnp.maximum(logs[0], logs[1]), jnp.maximum(logs[2], logs[3]))
    shares = [jnp.exp2(log - best) for log in logs]
    inverse = 1.0 / (shares[0] + shares[1] + shares[2] + shares[3])
    table = jnp.concatenate(
        [share * inverse for share in shares] + [jnp.zeros((128 - 32, ROWS), F32)], axis=0
    ).T
    for h in range(HEADS_Q):
        cols = slice(h * HD, (h + 1) * HD)
        total = jnp.zeros((ROWS, HD), F32)
        for i, ref in enumerate(refs):
            total += table[:, 8 * i + h : 8 * i + h + 1] * ref[:ROWS, cols].astype(F32)
        out_ref[:, cols] = total.astype(BF16)


def call(kernel, name, out_shape, in_specs, limit, flops, moved, streamed=False, **options):
    out_specs = jax.tree.map(lambda _: VM, out_shape)
    if streamed:
        options["grid"] = (1,)
        in_specs = [
            spec if spec in (SM, ANY) else pl.BlockSpec(spec, lambda i, n=len(spec): (0,) * n)
            for spec in in_specs
        ]
        out_specs = jax.tree.map(
            lambda out: pl.BlockSpec(out.shape, lambda i, n=len(out.shape): (0,) * n), out_shape
        )
    return pl.pallas_call(
        kernel,
        out_shape=out_shape,
        in_specs=in_specs,
        out_specs=out_specs,
        name=name,
        cost_estimate=pl.CostEstimate(flops=flops, bytes_accessed=moved, transcendentals=0),
        compiler_params=pltpu.CompilerParams(vmem_limit_bytes=limit * MIB),
        **options,
    )


def shape(dims, kind):
    return jax.ShapeDtypeStruct(dims, kind)


def swap(value, axis, size, step):
    return lax.ppermute(value, axis, [(i, i ^ step) for i in range(size)])


def exchange(chunks, axes):
    return lax.all_to_all(chunks, axes, 0, 0, tiled=True)


def after(kernel, inputs):
    def ordered(*refs):
        kernel(*refs[:inputs], *refs[inputs + 1 :])

    return ordered


def body(
    hidden_states,
    ssm_input,
    step_size,
    decay_rate,
    proj_b,
    proj_c,
    skip_gain,
    norm_gain,
    latent_from_ssm,
    latent_from_hidden,
    key_rebuild,
    value_rebuild,
    queries,
):
    place = jnp.stack(
        [lax.axis_index(axis) for axis in ("y", "x", "z", "core")]
    ).astype(jnp.int32)

    payload = call(
        state_kernel,
        "state",
        shape((NX, STATE, PAY), BF16),
        [SM, (ROWS, INNER), (HEADS_SSM, ROWS), (STATE, ROWS)],
        60,
        1 << 27,
        MIB,
        streamed=True,
    )(decay_rate, ssm_input, step_size, proj_b)
    spans = exchange(payload, "x")
    from_hidden = call(
        after(hidden_kernel, 2),
        "hidden",
        shape((ROWS, RANK), F32),
        [VM, VM, ANY],
        16,
        1 << 31,
        MIB,
    )(hidden_states, latent_from_hidden, payload)
    totals, before, row_decay = call(
        after(row_kernel, 2),
        "row",
        (
            shape((NY, STATE, PAY), BF16),
            shape((STATE, INNER), F32),
            shape((STATE, INNER), F32),
        ),
        [SM, VM, ANY],
        8,
        1 << 24,
        MIB // 2,
    )(place, spans, from_hidden)

    rows = exchange(totals, "y")
    partial, growth = call(
        after(intra_kernel, 6),
        "intra",
        (shape((ROWS, INNER), F32), shape((ROWS, 128), BF16)),
        [SM, SM] + [VM] * 4 + [ANY],
        24,
        1 << 31,
        3 * MIB,
    )(decay_rate, skip_gain, ssm_input, step_size, proj_b, proj_c, before)
    mamba_out, latent_terms = call(
        finish_kernel,
        "finish",
        (shape((ROWS, INNER), BF16), shape((ROWS, RANK), BF16)),
        [SM] + [VM] * 9,
        24,
        1 << 29,
        4 * MIB,
    )(
        place, rows, before, row_decay, partial, growth, proj_c, norm_gain.reshape(1, INNER),
        latent_from_ssm, from_hidden,
    )

    def copied(done):
        return call(
            after(copy_kernel, 1), "copy", shape(queries.shape, BF16), [VM, ANY], 8, 1 << 27, MIB
        )(queries, done)

    pieces = exchange(latent_terms.reshape(NT, PIECE, RANK), ("z", "core"))
    lent = copied(latent_terms)
    latents = call(
        after(sum_kernel, 1),
        "sum",
        shape((NY * NZ, PIECE, RANK), BF16),
        [VM, ANY],
        8,
        1 << 20,
        MIB // 2,
    )(pieces, lent)

    blocks = exchange(latents, ("y", "z")).reshape(NY, HALF, RANK)
    lent = copied(latents)
    visiting1, visiting2, visiting3 = [swap(lent, "x", NX, k) for k in (1, 2, 3)]
    weights = pl.pallas_call(
        weights_kernel,
        out_shape=shape((RANK, 2 * HD), BF16),
        grid_spec=pltpu.PrefetchScalarGridSpec(
            num_scalar_prefetch=1,
            grid=(1,),
            in_specs=[pl.BlockSpec((RANK, HD), lambda i, place: (0, place[2]))] * 2 + [ANY],
            out_specs=pl.BlockSpec((RANK, 2 * HD), lambda i, place: (0, 0)),
        ),
        name="weights",
        cost_estimate=pl.CostEstimate(flops=1 << 30, bytes_accessed=MIB, transcendentals=0),
        compiler_params=pltpu.CompilerParams(vmem_limit_bytes=8 * MIB),
    )(place, key_rebuild, value_rebuild, latents)
    mine = call(
        after(after(after(rebuild_kernel, 3), 3), 3),
        "rebuild",
        shape((NY * HALF, 2 * HD), BF16),
        [SM, VM, VM, ANY, ANY, ANY],
        8,
        1 << 27,
        MIB,
    )(place, blocks, weights, visiting1, visiting2, visiting3)
    other = swap(mine, "core", NC, 1)

    work = 4 * ROWS * HEADS_Q * HD * NY * ROWS
    answer = shape((ROWS + 16, HEADS_Q * HD), BF16)
    wide = shape((NY * ROWS, 2 * HD), BF16)
    done, keys, values = call(
        functools.partial(attend_first_kernel, 2), "attend", (answer, wide, wide),
        [SM, VM, VM, VM], 24, work, 4 * MIB,
    )(place, visiting2, mine, other)
    back = {2: swap(done, "x", NX, 2)}
    for step, query, awaited in ((1, visiting1, None), (3, visiting3, None), (0, queries, 2)):
        kernel = functools.partial(attend_kernel, step)
        operands = [place, query, keys, values, done]
        if awaited is not None:
            operands.append(back[awaited])
            kernel = after(kernel, 4)
        done = call(
            after(kernel, 4), "attend", answer, [SM, VM, VM, VM] + [ANY] * (len(operands) - 4),
            24, work, 4 * MIB,
        )(*operands)
        if step:
            back[step] = swap(done, "x", NX, step)

    attended = call(
        combine_kernel,
        "combine",
        shape((ROWS, HEADS_Q * HD), BF16),
        [VM] * 4,
        16,
        1 << 20,
        2 * MIB,
    )(done, back[1], back[2], back[3])
    return (mamba_out, attended)


def solution(mesh):
    grid = Mesh(mesh.devices.reshape(NY, NX, NZ, NC), ("y", "x", "z", "core"))
    ctx, tp = ("y", "x"), ("z", "core")
    return jax.shard_map(
        body,
        mesh=grid,
        in_specs=(
            P(ctx, tp),
            P(ctx, tp),
            P(tp, ctx),
            P(tp),
            P(None, ctx),
            P(None, ctx),
            P(tp),
            P(tp),
            P(tp, None),
            P(tp, None),
            P(),
            P(),
            P(ctx, tp),
        ),
        out_specs=(P(ctx, tp), P(ctx, tp)),
        check_vma=False,
    )
```

```python
import functools
import math

import jax
import jax.numpy as jnp
from jax import lax
from jax.experimental import pallas as pl
from jax.experimental.pallas import tpu as pltpu
from jax.sharding import Mesh
from jax.sharding import PartitionSpec as P

STATE = 16
HEADDIM = 64
ROWS = 256
HEADS_SSM = 16
INNER = HEADS_SSM * HEADDIM
HD = 128
RANK = 256
HEADS_Q = 4
NY, NX, NZ, NC = 8, 4, 8, 2
NT = NZ * NC
PIECE = ROWS // NT
HALF = ROWS // NC
NCTX = NY * NX
PAY = INNER + 128
BLOCKS = INNER // 128

NEG_BIG = -1e30
EPSILON = 1e-05
SCALE2 = math.log2(math.e) / math.sqrt(HD)
F32 = jnp.float32
BF16 = jnp.bfloat16
MIB = 1 << 20

VM = pl.BlockSpec(memory_space=pltpu.VMEM)
ANY = pl.BlockSpec(memory_space=pl.ANY)
SM = pl.BlockSpec(memory_space=pltpu.SMEM)


def iota(shape, axis):
    return lax.broadcasted_iota(jnp.int32, shape, axis)


def dot(a, b):
    return jnp.dot(a, b, preferred_element_type=F32)


def split(value):
    high = value.astype(BF16)
    return high, (value - high.astype(F32)).astype(BF16)


def spread():
    lane = iota((128, INNER), 0)
    head = iota((128, INNER), 1) // HEADDIM
    return jnp.where((lane < 2 * HEADS_SSM) & ((lane & 15) == head), 1.0, 0.0).astype(BF16)


def within_rows(step_ref, rate_ref):
    row = iota((HEADS_SSM, ROWS), 0)
    lane = iota((HEADS_SSM, ROWS), 1)
    rate = jnp.zeros((HEADS_SSM, ROWS), F32)
    for h in range(HEADS_SSM):
        rate = jnp.where(row == h, rate_ref[h], rate)
    total = -rate * step_ref[...]
    shift = 1
    while shift < ROWS:
        total = total + jnp.where(lane >= shift, pltpu.roll(total, shift, 1), 0.0)
        shift *= 2
    return total


def pack_decay(compact):
    lane = iota(compact.shape, 1)
    kept = jnp.where(lane < HEADS_SSM, compact, 0.0)
    high = kept.astype(BF16).astype(F32)
    low = pltpu.roll(kept - high, HEADS_SSM, 1)
    return (high + low).astype(BF16)


def unpack_decay(packed):
    value = packed.astype(F32)
    lane = iota(value.shape, 1)
    return jnp.where(lane < HEADS_SSM, value + pltpu.roll(value, 128 - HEADS_SSM, 1), 0.0)


def state_kernel(rate_ref, x_ref, step_ref, b_ref, pay_ref):
    within = within_rows(step_ref, rate_ref)
    last = within[:, ROWS - 1 : ROWS]
    to_end = jnp.exp(last - within)
    b = b_ref[...].astype(F32)
    lane = iota((STATE, 128), 1)
    for j in range(BLOCKS):
        cols = slice(128 * j, 128 * (j + 1))
        a0h, a0l = split(to_end[2 * j : 2 * j + 1, :] * b)
        a1h, a1l = split(to_end[2 * j + 1 : 2 * j + 2, :] * b)
        lhs = jnp.concatenate([a0h, a1h, a0l, a1l], axis=0)
        out = dot(lhs, x_ref[:, cols])
        both = out[: 2 * STATE] + out[2 * STATE :]
        state = jnp.where(lane < HEADDIM, both[:STATE], both[STATE:])
        for i in range(NX):
            pay_ref[i, :, cols] = state.astype(BF16)
    head = iota((HEADS_SSM, 128), 0)
    hlane = iota((HEADS_SSM, 128), 1)
    compact = jnp.sum(jnp.where(hlane == head, jnp.exp(last), 0.0), axis=0, keepdims=True)
    packed = pack_decay(jnp.broadcast_to(compact, (STATE, 128)))
    for i in range(NX):
        pay_ref[i, :, INNER:] = packed


def widened(spans_ref, count):
    packed = jnp.concatenate([spans_ref[i, :, INNER:] for i in range(count)], axis=0)
    wide = dot(packed, spread())
    return [wide[i * STATE : (i + 1) * STATE] for i in range(count)]


def row_kernel(place_ref, spans_ref, total_ref, before_ref, decay_ref):
    x = place_ref[1]
    wide = widened(spans_ref, NX)
    run = jnp.zeros((STATE, INNER), F32)
    before = run
    before_decay = jnp.ones((STATE, INNER), F32)
    compact = jnp.ones((STATE, 128), F32)
    for i in range(NX):
        run = wide[i] * run + spans_ref[i, :, :INNER].astype(F32)
        before = jnp.where(i < x, run, before)
        before_decay = jnp.where(i < x, wide[i] * before_decay, before_decay)
        compact = compact * unpack_decay(spans_ref[i, :, INNER:])
    before_ref[...] = before
    decay_ref[...] = before_decay
    total = run.astype(BF16)
    packed = pack_decay(compact)
    for i in range(NY):
        total_ref[i, :, :INNER] = total
        total_ref[i, :, INNER:] = packed


def intra_kernel(
    rate_ref, skip_ref, x_ref, step_ref, b_ref, c_ref, y_ref, grow_ref
):
    within = within_rows(step_ref, rate_ref)
    columns = jnp.concatenate([within, jnp.zeros((128 - HEADS_SSM, ROWS), F32)], axis=0).T
    grow = jnp.exp(columns)
    grow_ref[...] = pack_decay(grow)
    meet = lax.dot_general(
        c_ref[...], b_ref[...], (((0,), (0,)), ((), ())), preferred_element_type=F32
    )
    half = ROWS // 2
    causal = iota((half, half), 0) >= iota((half, half), 1)
    lane = iota((ROWS, 128), 1)
    zeros = jnp.zeros((half, half), BF16)

    def mixing(h):
        row = within[h : h + 1, :]
        column = columns[:, h : h + 1]
        top, bottom = column[:half], column[half:]
        left, right = row[:, :half], row[:, half:]
        m00 = meet[:half, :half] * jnp.exp(jnp.where(causal, top - left, NEG_BIG))
        m10 = meet[half:, :half] * jnp.exp(bottom - left)
        m11 = meet[half:, half:] * jnp.exp(jnp.where(causal, bottom - right, NEG_BIG))
        upper = jnp.concatenate([m00.astype(BF16), zeros], axis=1)
        lower = jnp.concatenate([m10.astype(BF16), m11.astype(BF16)], axis=1)
        return jnp.concatenate([upper, lower], axis=0)

    for j in range(HEADS_SSM // 2):
        cols = slice(128 * j, 128 * (j + 1))
        x = x_ref[:, cols]
        out0 = dot(mixing(2 * j), x)
        out1 = dot(mixing(2 * j + 1), x)
        skip = jnp.where(lane < HEADDIM, skip_ref[2 * j], skip_ref[2 * j + 1])
        y_ref[:, cols] = jnp.where(lane < HEADDIM, out0, out1) + skip * x.astype(F32)


def finish_kernel(
    place_ref, rows_ref, before_ref, decay_ref, y_ref, grow_ref, c_ref, gain_ref, w_ref, h_ref,
    mamba_ref, part_ref,
):
    chan = spread()
    wide = widened(rows_ref, NY - 1)
    run = jnp.zeros((STATE, INNER), F32)
    for row in range(NY - 1):
        joined = wide[row] * run + rows_ref[row, :, :INNER].astype(F32)
        run = jnp.where(row < place_ref[0], joined, run)
    carried = run * decay_ref[...] + before_ref[...]
    high, low = split(carried)
    c = c_ref[...]
    from_state = lax.dot_general(
        jnp.concatenate([c, c], axis=0),
        jnp.concatenate([high, low], axis=0),
        (((0,), (0,)), ((), ())),
        preferred_element_type=F32,
    )
    grow = dot(grow_ref[...], chan)
    out = y_ref[...] + from_state * grow
    gather = jnp.where(
        iota((INNER, 128), 0) // HEADDIM == iota((INNER, 128), 1), 1.0, 0.0
    ).astype(BF16)
    square = dot((out * out).astype(BF16), gather) * (1.0 / HEADDIM)
    inverse = dot(pack_decay(lax.rsqrt(square + EPSILON)), chan)
    mamba = (out * inverse * gain_ref[...]).astype(BF16)
    mamba_ref[...] = mamba
    part_ref[...] = (dot(mamba, w_ref[...]) + h_ref[...]).astype(BF16)


def copy_kernel(q_ref, out_ref):
    out_ref[...] = q_ref[...]


def sum_kernel(pieces_ref, out_ref):
    total = pieces_ref[0].astype(F32)
    for i in range(1, NT):
        total = total + pieces_ref[i].astype(F32)
    rounded = total.astype(BF16)
    for i in range(NY * NZ):
        out_ref[i] = rounded


def hidden_kernel(hidden_ref, w_ref, out_ref):
    out_ref[...] = dot(hidden_ref[...], w_ref[...])


def weights_kernel(place_ref, wk_ref, wv_ref, order_ref, out_ref):
    out_ref[:, :HD] = wk_ref[...]
    out_ref[:, HD:] = wv_ref[...]


def rebuild_kernel(place_ref, mine_ref, w_ref, out_ref):
    y = place_ref[0]
    w = w_ref[...]
    for block in range(NY):
        begin = ((y - block) & (NY - 1)) * HALF
        out = pl.ds(pl.multiple_of(begin, HALF), HALF)
        rows = dot(mine_ref[block], w)
        out_ref[out, :HD] = (rows[:, :HD] * SCALE2).astype(BF16)
        out_ref[out, HD:] = rows[:, HD:].astype(BF16)


def place_keys(y, mine_ref, other_ref, k_ref, v_ref):
    row = iota((HD, HALF), 0)
    ones = jnp.ones((HALF, HD), BF16)
    for part, ref in enumerate((mine_ref, other_ref)):
        for block in range(NY):
            rows = slice(block * HALF, (block + 1) * HALF)
            out = slice((part * NY + block) * HALF, (part * NY + block + 1) * HALF)
            bias = jnp.where(y >= block, 0.0, NEG_BIG)
            near = 1.0 if block == 0 else 0.0
            k_ref[:HD, out] = ref[rows, :HD].astype(F32).T.astype(BF16)
            k_ref[HD:, out] = jnp.where(row == 0, bias, jnp.where(row == 1, near, 0.0)).astype(
                BF16
            )
            v_ref[out, :HD] = ref[rows, HD:]
            v_ref[out, HD:] = ones


def own_masked(scores, core):
    token = iota((2 * ROWS, HALF), 0) & (ROWS - 1)
    slot = iota((2 * ROWS, HALF), 1)
    pieces = []
    for part, own in enumerate((core, 1 - core)):
        key = (slot // PIECE) * (2 * PIECE) + own * PIECE + (slot & (PIECE - 1))
        begin = part * NY * HALF
        pieces.append(jnp.where(key <= token, scores[:, begin : begin + HALF], NEG_BIG))
        pieces.append(scores[:, begin + HALF : begin + NY * HALF])
    return jnp.concatenate(pieces, axis=1)


def attend_kernel(step, place_ref, q_ref, k_ref, v_ref, out_ref):
    x, core = place_ref[1], place_ref[3]
    lane = iota((ROWS, 128), 1)
    behind = jnp.where((x ^ step) < x, NEG_BIG, 0.0)
    unit = jnp.where(lane == 0, 1.0, jnp.where(lane == 1, behind, 0.0)).astype(BF16)

    def scored(first):
        query = jnp.concatenate(
            [
                jnp.concatenate([q_ref[:, h * HD : (h + 1) * HD], unit], axis=1)
                for h in (first, first + 1)
            ],
            axis=0,
        )
        return dot(query, k_ref[...])

    stats = jnp.zeros((ROWS, 128), F32)
    following = scored(0)
    for first in range(0, HEADS_Q, 2):
        scores = following
        if first + 2 < HEADS_Q:
            following = scored(first + 2)
        if step == 0:
            scores = own_masked(scores, core)
        best = jnp.max(scores, axis=1, keepdims=True)
        weights = jnp.exp2(scores - best).astype(BF16)
        sums = dot(weights, v_ref[...])
        norm = sums[:, HD:]
        ratio = (sums[:, :HD] / norm).astype(BF16)
        level = best + jnp.log2(norm)
        for h in (first, first + 1):
            rows = slice((h - first) * ROWS, (h - first + 1) * ROWS)
            out_ref[:ROWS, h * HD : (h + 1) * HD] = ratio[rows]
            stats = jnp.where(lane == h, level[rows], stats)
    rows = stats.T[:8, :]
    high, mid = split(rows)
    low = (rows - high.astype(F32) - mid.astype(F32)).astype(BF16)
    upper = jnp.concatenate([high, mid], axis=1)
    lower = jnp.concatenate([low, jnp.zeros((8, ROWS), BF16)], axis=1)
    out_ref[ROWS:, :] = jnp.concatenate([upper, lower], axis=0)


def attend_first_kernel(step, place_ref, q_ref, mine_ref, other_ref, out_ref, k_ref, v_ref):
    place_keys(place_ref[0], mine_ref, other_ref, k_ref, v_ref)
    attend_kernel(step, place_ref, q_ref, k_ref, v_ref, out_ref)


def combine_kernel(own_ref, back1_ref, back2_ref, back3_ref, out_ref):
    refs = [own_ref, back1_ref, back2_ref, back3_ref]
    logs = []
    for ref in refs:
        tail = ref[ROWS:, :].astype(F32)
        logs.append(tail[:8, :ROWS] + tail[:8, ROWS:] + tail[8:, :ROWS])
    best = jnp.maximum(jnp.maximum(logs[0], logs[1]), jnp.maximum(logs[2], logs[3]))
    shares = [jnp.exp2(log - best) for log in logs]
    inverse = 1.0 / (shares[0] + shares[1] + shares[2] + shares[3])
    table = jnp.concatenate(
        [share * inverse for share in shares] + [jnp.zeros((128 - 32, ROWS), F32)], axis=0
    ).T
    for h in range(HEADS_Q):
        cols = slice(h * HD, (h + 1) * HD)
        total = jnp.zeros((ROWS, HD), F32)
        for i, ref in enumerate(refs):
            total += table[:, 8 * i + h : 8 * i + h + 1] * ref[:ROWS, cols].astype(F32)
        out_ref[:, cols] = total.astype(BF16)


def call(kernel, name, out_shape, in_specs, limit, flops, moved, streamed=False, **options):
    out_specs = jax.tree.map(lambda _: VM, out_shape)
    if streamed:
        options["grid"] = (1,)
        in_specs = [
            spec if spec in (SM, ANY) else pl.BlockSpec(spec, lambda i, n=len(spec): (0,) * n)
            for spec in in_specs
        ]
        out_specs = jax.tree.map(
            lambda out: pl.BlockSpec(out.shape, lambda i, n=len(out.shape): (0,) * n), out_shape
        )
    return pl.pallas_call(
        kernel,
        out_shape=out_shape,
        in_specs=in_specs,
        out_specs=out_specs,
        name=name,
        cost_estimate=pl.CostEstimate(flops=flops, bytes_accessed=moved, transcendentals=0),
        compiler_params=pltpu.CompilerParams(vmem_limit_bytes=limit * MIB),
        **options,
    )


def shape(dims, kind):
    return jax.ShapeDtypeStruct(dims, kind)


def swap(value, axis, size, step):
    return lax.ppermute(value, axis, [(i, i ^ step) for i in range(size)])


def exchange(chunks, axes):
    return lax.all_to_all(chunks, axes, 0, 0, tiled=True)


def after(kernel, inputs):
    def ordered(*refs):
        kernel(*refs[:inputs], *refs[inputs + 1 :])

    return ordered


def body(
    hidden_states,
    ssm_input,
    step_size,
    decay_rate,
    proj_b,
    proj_c,
    skip_gain,
    norm_gain,
    latent_from_ssm,
    latent_from_hidden,
    key_rebuild,
    value_rebuild,
    queries,
):
    place = jnp.stack(
        [lax.axis_index(axis) for axis in ("y", "x", "z", "core")]
    ).astype(jnp.int32)

    payload = call(
        state_kernel,
        "state",
        shape((NX, STATE, PAY), BF16),
        [SM, (ROWS, INNER), (HEADS_SSM, ROWS), (STATE, ROWS)],
        60,
        1 << 27,
        MIB,
        streamed=True,
    )(decay_rate, ssm_input, step_size, proj_b)
    spans = exchange(payload, "x")
    from_hidden = call(
        after(hidden_kernel, 2),
        "hidden",
        shape((ROWS, RANK), F32),
        [VM, VM, ANY],
        16,
        1 << 31,
        MIB,
    )(hidden_states, latent_from_hidden, payload)
    totals, before, row_decay = call(
        after(row_kernel, 2),
        "row",
        (
            shape((NY, STATE, PAY), BF16),
            shape((STATE, INNER), F32),
            shape((STATE, INNER), F32),
        ),
        [SM, VM, ANY],
        8,
        1 << 24,
        MIB // 2,
    )(place, spans, from_hidden)

    rows = exchange(totals, "y")
    partial, growth = call(
        after(intra_kernel, 6),
        "intra",
        (shape((ROWS, INNER), F32), shape((ROWS, 128), BF16)),
        [SM, SM] + [VM] * 4 + [ANY],
        24,
        1 << 31,
        3 * MIB,
    )(decay_rate, skip_gain, ssm_input, step_size, proj_b, proj_c, before)
    mamba_out, latent_terms = call(
        finish_kernel,
        "finish",
        (shape((ROWS, INNER), BF16), shape((ROWS, RANK), BF16)),
        [SM] + [VM] * 9,
        24,
        1 << 29,
        4 * MIB,
    )(
        place, rows, before, row_decay, partial, growth, proj_c, norm_gain.reshape(1, INNER),
        latent_from_ssm, from_hidden,
    )

    def copied(done):
        return call(
            after(copy_kernel, 1), "copy", shape(queries.shape, BF16), [VM, ANY], 8, 1 << 27, MIB
        )(queries, done)

    pieces = exchange(latent_terms.reshape(NT, PIECE, RANK), ("z", "core"))
    lent = copied(latent_terms)
    latents = call(
        after(sum_kernel, 1),
        "sum",
        shape((NY * NZ, PIECE, RANK), BF16),
        [VM, ANY],
        8,
        1 << 20,
        MIB // 2,
    )(pieces, lent)

    blocks = exchange(latents, ("y", "z")).reshape(NY, HALF, RANK)
    lent = copied(latents)
    visiting1, visiting2, visiting3 = [swap(lent, "x", NX, k) for k in (1, 2, 3)]
    weights = pl.pallas_call(
        weights_kernel,
        out_shape=shape((RANK, 2 * HD), BF16),
        grid_spec=pltpu.PrefetchScalarGridSpec(
            num_scalar_prefetch=1,
            grid=(1,),
            in_specs=[pl.BlockSpec((RANK, HD), lambda i, place: (0, place[2]))] * 2 + [ANY],
            out_specs=pl.BlockSpec((RANK, 2 * HD), lambda i, place: (0, 0)),
        ),
        name="weights",
        cost_estimate=pl.CostEstimate(flops=1 << 30, bytes_accessed=MIB, transcendentals=0),
        compiler_params=pltpu.CompilerParams(vmem_limit_bytes=8 * MIB),
    )(place, key_rebuild, value_rebuild, latents)
    mine = call(
        after(after(after(rebuild_kernel, 3), 3), 3),
        "rebuild",
        shape((NY * HALF, 2 * HD), BF16),
        [SM, VM, VM, ANY, ANY, ANY],
        8,
        1 << 27,
        MIB,
    )(place, blocks, weights, visiting1, visiting2, visiting3)
    other = swap(mine, "core", NC, 1)

    work = 4 * ROWS * HEADS_Q * HD * NY * ROWS
    answer = shape((ROWS + 16, HEADS_Q * HD), BF16)
    columns, wide = shape((2 * HD, NY * ROWS), BF16), shape((NY * ROWS, 2 * HD), BF16)
    done, keys, values = call(
        functools.partial(attend_first_kernel, 2), "attend", (answer, columns, wide),
        [SM, VM, VM, VM], 24, work, 4 * MIB,
    )(place, visiting2, mine, other)
    back = {2: swap(done, "x", NX, 2)}
    for step, query, awaited in ((1, visiting1, None), (3, visiting3, None), (0, queries, 2)):
        kernel = functools.partial(attend_kernel, step)
        operands = [place, query, keys, values, done]
        if awaited is not None:
            operands.append(back[awaited])
            kernel = after(kernel, 4)
        done = call(
            after(kernel, 4), "attend", answer, [SM, VM, VM, VM] + [ANY] * (len(operands) - 4),
            24, work, 4 * MIB,
        )(*operands)
        if step:
            back[step] = swap(done, "x", NX, step)

    attended = call(
        combine_kernel,
        "combine",
        shape((ROWS, HEADS_Q * HD), BF16),
        [VM] * 4,
        16,
        1 << 20,
        2 * MIB,
    )(done, back[1], back[2], back[3])
    return (mamba_out, attended)


def solution(mesh):
    grid = Mesh(mesh.devices.reshape(NY, NX, NZ, NC), ("y", "x", "z", "core"))
    ctx, tp = ("y", "x"), ("z", "core")
    return jax.shard_map(
        body,
        mesh=grid,
        in_specs=(
            P(ctx, tp),
            P(ctx, tp),
            P(tp, ctx),
            P(tp),
            P(None, ctx),
            P(None, ctx),
            P(tp),
            P(tp),
            P(tp, None),
            P(tp, None),
            P(),
            P(),
            P(ctx, tp),
        ),
        out_specs=(P(ctx, tp), P(ctx, tp)),
        check_vma=False,
    )
```
